32 devices in a mesh: sx: 2 (over y), sy: 4 (over z), vel: 4 (over x, core).
Axes of the slice: x: 2, y: 2, z: 4, core: 2. Of those that a mesh axis runs over, the one named last changes fastest.
Arguments:
- distribution: float32 [32, 128, 13824], P('sx', 'sy', 'vel'), as said below
- cell_kind: int32 [32, 128], P('sx', 'sy'), may hold values from 0 to 2, as said below
- local_knudsen: float32 [32, 128], P('sx', 'sy'), may hold values from 0.3 to 30
Outputs:
- evolved: float32 [32, 128, 13824], P('sx', 'sy', 'vel')
The draws below stay inside these ranges and needn't reach their ends.
Inputs may be any that keep to these rules, and one draw needn't show every extreme that they name: `cell_kind`: 0 marks a gas cell, 1 a wall cell, 2 an inflow cell. `distribution`: every entry is positive.
All inputs are finite; a program needn't handle non-finite values.
Results may differ from the reference program's by a relative error of at most 0.0003.
Values sent between devices are 32-bit elements; how exact they have to be, the bound alone decides.
A program may use at most 128 MiB of HBM per device.

```python
import math
import jax
import jax.numpy as jnp
from jax import lax

NVX = 24
STEPS = 2
NX = 32
NY = 128
N_VEL = 4


VEL_LIMIT = 4.8


def draw_distribution(key, part):
    key = jax.random.fold_in(key, 11)
    sampler_seeds = jax.random.split(key, 8)
    lattice_slice_xy = (NX, NY)
    molecule_crowding = jnp.exp(jax.random.uniform(sampler_seeds[0], lattice_slice_xy, jnp.float32, math.log(8.0), math.log(24.0)))
    noise = jax.random.uniform(sampler_seeds[6], (NX, NY, NVX ** 3), jnp.float32, -1.0, 1.0)
    mean_motion_x = jax.random.uniform(sampler_seeds[1], lattice_slice_xy, jnp.float32, -0.6, 0.6)[..., None]
    mean_motion_y = jax.random.uniform(sampler_seeds[2], lattice_slice_xy, jnp.float32, -0.4, 0.4)[..., None]
    mean_motion_z = jax.random.uniform(sampler_seeds[3], lattice_slice_xy, jnp.float32, -0.2, 0.2)[..., None]
    molecular_agitation = jax.random.uniform(sampler_seeds[4], lattice_slice_xy, jnp.float32, 0.7, 1.4)[..., None]
    ripple_magnitude = jax.random.uniform(sampler_seeds[5], lattice_slice_xy, jnp.float32, -1.0, 1.0)[..., None]
    spacing = 2.0 * VEL_LIMIT / NVX
    points = jnp.arange(NVX, dtype=jnp.int32)
    line = ((points // 2).astype(jnp.float32) + 0.5) * spacing * (2 * (points % 2) - 1).astype(jnp.float32)
    relative_motion_component = jnp.tile(line, NVX * NVX) - mean_motion_x
    drift_y = jnp.tile(jnp.repeat(line, NVX), NVX) - mean_motion_y
    drift_z = jnp.repeat(line, NVX * NVX) - mean_motion_z
    relative_motion_norm = relative_motion_component * relative_motion_component + drift_y * drift_y + drift_z * drift_z
    maxwell_profile = molecule_crowding[..., None] / (2.0 * math.pi * molecular_agitation) ** 1.5 * jnp.exp(-relative_motion_norm / (2.0 * molecular_agitation))
    extent_tuple = jnp.exp(0.3 * ripple_magnitude * jnp.tanh(relative_motion_component * (relative_motion_norm / molecular_agitation - 5.0) / 10.0))
    return maxwell_profile * extent_tuple * (1.0 + 0.4 * noise)


def draw_cell_kind(key, part):
    key = jax.random.fold_in(key, 23)
    sampler_seeds = jax.random.split(key, 5)
    number = 6
    centre_x = jax.random.randint(sampler_seeds[0], (number,), 0, NX)
    centre_y = jax.random.randint(sampler_seeds[1], (number,), 0, NY)
    half_x = jax.random.randint(sampler_seeds[2], (number,), 1, 2 + NX // 16)
    half_y = jax.random.randint(sampler_seeds[3], (number,), 1, 2 + NY // 16)
    rows = jnp.arange(NX, dtype=jnp.int32)[:, None, None]
    columns = jnp.arange(NY, dtype=jnp.int32)[None, :, None]
    apart_x = jnp.abs(rows - centre_x)
    apart_x = jnp.minimum(apart_x, NX - apart_x)
    apart_y = jnp.abs(columns - centre_y)
    apart_y = jnp.minimum(apart_y, NY - apart_y)
    wall = jnp.any((apart_x <= half_x) & (apart_y <= half_y), axis=-1)
    band = jax.random.randint(sampler_seeds[4], (), 0, NX)
    inflow = ((jnp.arange(NX, dtype=jnp.int32) - band) % NX < 2)[:, None]
    return jnp.where(inflow, 2, jnp.where(wall, 1, 0)).astype(jnp.int32)


def level_of(stream_key, shape, pieces, least, largest):
    factor_of = 1.0
    for dim, shards_of in pieces:
        draws = jax.random.uniform(jax.random.fold_in(jax.random.fold_in(stream_key, 6), dim), (shards_of,), jnp.float32, least / len(pieces), largest / len(pieces))
        factor_of = factor_of * jnp.repeat(jnp.exp(draws), shape[dim] // shards_of).reshape((-1,) + (1,) * (len(shape) - 1 - dim))
    return factor_of


def setup_inputs(seed: int = 0) -> dict:
    arg_keys = jax.random.split(jax.random.key(seed), 4)
    return {
        "distribution": draw_distribution(jax.random.fold_in(arg_keys[3], 71), 0),
        "cell_kind": draw_cell_kind(jax.random.fold_in(arg_keys[3], 71), 0),
        "local_knudsen": jnp.clip(jnp.exp(math.log(30.0) - 4.6051701 * jax.random.uniform(arg_keys[2], (NX, NY), jnp.float32) ** level_of(arg_keys[2], (NX, NY), ((0, 2), (1, 4)), -0.2, 0.2)), 0.3, 30.0),
    }


VEL_LIMIT = 4.8
CLOCK_ADVANCE = 0.09
VISCOUS_RATIO = 2.0 / 3.0
WALL_TEMP = 1.0
INFLOW_DENSITY = 12.0
INFLOW_SPEED = 0.5
INFLOW_TEMP = 1.0

def velocity_grid():
    spacing = 2.0 * VEL_LIMIT / NVX
    points = jnp.arange(NVX, dtype=jnp.int32)
    line = ((points // 2).astype(jnp.float32) + 0.5) * spacing * (2 * (points % 2) - 1).astype(jnp.float32)
    speed_x = jnp.tile(line, NVX * NVX)
    speed_y = jnp.tile(jnp.repeat(line, NVX), NVX)
    speed_z = jnp.repeat(line, NVX * NVX)
    return (speed_x, speed_y, speed_z, spacing ** 3)

def widen_last_index(value):
    return value[..., None]

def conserved_integrals(quadrature_totals):
    molecule_crowding = quadrature_totals[0]
    mean_motion_x = quadrature_totals[1] / molecule_crowding
    mean_motion_y = quadrature_totals[2] / molecule_crowding
    mean_motion_z = quadrature_totals[3] / molecule_crowding
    molecular_agitation = (quadrature_totals[4] / molecule_crowding - (mean_motion_x * mean_motion_x + mean_motion_y * mean_motion_y + mean_motion_z * mean_motion_z)) / 3.0
    return (molecule_crowding, mean_motion_x, mean_motion_y, mean_motion_z, molecular_agitation)

def relax(present_state, macro_integrals, local_knudsen, cell_kind, speed_x, speed_y, speed_z):
    molecule_crowding, mean_motion_x, mean_motion_y, mean_motion_z, molecular_agitation, conduction_x, conduction_y, conduction_z = macro_integrals
    relative_motion_component = speed_x - widen_last_index(mean_motion_x)
    drift_y = speed_y - widen_last_index(mean_motion_y)
    drift_z = speed_z - widen_last_index(mean_motion_z)
    relative_motion_norm = relative_motion_component * relative_motion_component + drift_y * drift_y + drift_z * drift_z
    maxwell_profile = widen_last_index(molecule_crowding / (2.0 * math.pi * molecular_agitation) ** 1.5) * jnp.exp(-relative_motion_norm / widen_last_index(2.0 * molecular_agitation))
    thermal_dot_offset = relative_motion_component * widen_last_index(conduction_x) + drift_y * widen_last_index(conduction_y) + drift_z * widen_last_index(conduction_z)
    leading_coefficient = (1.0 - VISCOUS_RATIO) * thermal_dot_offset / widen_last_index(5.0 * molecule_crowding * molecular_agitation * molecular_agitation) * (relative_motion_norm / widen_last_index(molecular_agitation) - 5.0)
    shakhov_closure_model = maxwell_profile * (1.0 + leading_coefficient)
    remaining_indicator = jnp.exp(-CLOCK_ADVANCE * molecule_crowding * jnp.sqrt(molecular_agitation) / local_knudsen)
    medium_cells = shakhov_closure_model + (present_state - shakhov_closure_model) * widen_last_index(remaining_indicator)
    speed_sq = speed_x * speed_x + speed_y * speed_y + speed_z * speed_z
    wall = widen_last_index(molecule_crowding / (2.0 * math.pi * WALL_TEMP) ** 1.5) * jnp.exp(-speed_sq / (2.0 * WALL_TEMP))
    shifted = speed_x - INFLOW_SPEED
    inflow = INFLOW_DENSITY / (2.0 * math.pi * INFLOW_TEMP) ** 1.5 * jnp.exp(-(shifted * shifted + speed_y * speed_y + speed_z * speed_z) / (2.0 * INFLOW_TEMP))
    return jnp.where(widen_last_index(cell_kind == 1), wall, jnp.where(widen_last_index(cell_kind == 2), inflow, medium_cells))

def minmod(left, right):
    return 0.5 * (jnp.sign(left) + jnp.sign(right)) * jnp.minimum(jnp.abs(left), jnp.abs(right))

def sweep_periodic(values, speed, axis):
    upper = jnp.roll(values, -1, axis)
    lower = jnp.roll(values, 1, axis)
    slope = minmod(values - lower, upper - values)
    forward = jnp.maximum(speed, 0.0)
    backward = jnp.minimum(speed, 0.0)
    right = forward * (values + 0.5 * slope) + backward * (upper - 0.5 * jnp.roll(slope, -1, axis))
    return right - jnp.roll(right, 1, axis)

def macroscopic(present_state, grid):
    speed_x, speed_y, speed_z, weight = grid
    basis = jnp.stack([jnp.ones_like(speed_x), speed_x, speed_y, speed_z, speed_x * speed_x + speed_y * speed_y + speed_z * speed_z]) * weight
    quadrature_totals = jnp.einsum('kv,xyv->kxy', basis, present_state, precision=lax.Precision.HIGHEST)
    molecule_crowding, mean_motion_x, mean_motion_y, mean_motion_z, molecular_agitation = conserved_integrals(quadrature_totals)
    width = NVX ** 3 // N_VEL

    def add_block(block_index, total):
        start = (block_index * width).astype(jnp.int32)
        piece = lax.dynamic_slice_in_dim(present_state, start, width, 2)
        relative_motion_component = lax.dynamic_slice_in_dim(speed_x, start, width, 0) - widen_last_index(mean_motion_x)
        drift_y = lax.dynamic_slice_in_dim(speed_y, start, width, 0) - widen_last_index(mean_motion_y)
        drift_z = lax.dynamic_slice_in_dim(speed_z, start, width, 0) - widen_last_index(mean_motion_z)
        relative_motion_norm = relative_motion_component * relative_motion_component + drift_y * drift_y + drift_z * drift_z
        return total + jnp.stack([lax.optimization_barrier(jnp.sum(relative_motion_component * relative_motion_norm * piece, axis=-1)), lax.optimization_barrier(jnp.sum(drift_y * relative_motion_norm * piece, axis=-1)), lax.optimization_barrier(jnp.sum(drift_z * relative_motion_norm * piece, axis=-1))])
    conduction_triple = lax.fori_loop(0, N_VEL, add_block, jnp.zeros((3, NX, NY), jnp.float32)) * (0.5 * weight)
    return (molecule_crowding, mean_motion_x, mean_motion_y, mean_motion_z, molecular_agitation, conduction_triple[0], conduction_triple[1], conduction_triple[2])

def advance(present_state, macro_integrals, local_knudsen, cell_kind, grid):
    speed_x, speed_y, speed_z, weight = grid
    width = NVX ** 3 // N_VEL

    def one_block(block_index, output):
        start = (block_index * width).astype(jnp.int32)
        piece = lax.dynamic_slice_in_dim(present_state, start, width, 2)
        part_x = lax.dynamic_slice_in_dim(speed_x, start, width, 0)
        part_y = lax.dynamic_slice_in_dim(speed_y, start, width, 0)
        part_z = lax.dynamic_slice_in_dim(speed_z, start, width, 0)
        relaxed = relax(piece, macro_integrals, local_knudsen, cell_kind, part_x, part_y, part_z)
        change = sweep_periodic(relaxed, part_x, 0) + sweep_periodic(relaxed, part_y, 1)
        return lax.dynamic_update_slice_in_dim(output, relaxed - CLOCK_ADVANCE * change, start, 2)
    return lax.fori_loop(0, N_VEL, one_block, jnp.zeros_like(present_state))

def reference(distribution, cell_kind, local_knudsen):
    grid = velocity_grid()
    present_state = distribution
    for section_index in range(STEPS):
        macro_integrals = macroscopic(present_state, grid)
        present_state = advance(present_state, macro_integrals, local_knudsen, cell_kind, grid)
    return present_state
```

```python
import functools
import math

import jax
import jax.numpy as jnp
from jax import lax
from jax.experimental import pallas as pl
from jax.experimental.pallas import tpu as pltpu
from jax.sharding import PartitionSpec as P

NVX = 24
STEPS = 2
VEL_LIMIT = 4.8
DT = 0.09
SPACING = 2.0 * VEL_LIMIT / NVX
HALF = 0.5 * SPACING
WEIGHT = SPACING**3
LANES = 128
PITCH = 48
TOP = 8
MESH = pl.DeviceIdType.MESH
F32 = jnp.float32
BF16 = jnp.bfloat16


def tables(index, valid):
    p = [index % NVX, index // NVX % NVX, index // (NVX * NVX)]
    m = [(2 * (q // 2) + 1) * (2 * (q % 2) - 1) for q in p]
    x, y, z = m
    sq = x * x + y * y + z * z
    quads = [x * x, y * y, z * z, x * y, x * z, y * z]
    cubes = [x * sq, y * sq, z * sq]
    q_hi = [(v + 8) // 16 * 16 for v in quads]
    c_hi = [(v + 128) // 256 * 256 for v in cubes]
    q_lo = [a - b for a, b in zip(quads, q_hi)]
    c_lo = [a - b for a, b in zip(cubes, c_hi)]
    one, zero = jnp.ones_like(x), jnp.zeros_like(x)
    rows = [one, x, y, z] + q_hi + c_hi + [zero] * 3 + [zero] * 4 + q_lo + c_lo + [zero] * 3
    phi = jnp.stack([jnp.where(valid, r, 0).astype(BF16) for r in rows], axis=1)
    speeds = [
        (x > 0).astype(F32),
        (y > 0).astype(F32),
        DT * HALF * jnp.abs(x).astype(F32),
        DT * HALF * jnp.abs(y).astype(F32),
    ]
    lane = jnp.stack(speeds + [jnp.zeros_like(speeds[0])] * 4, axis=1)
    return phi, lane


def coefficients(s, kind, kn):
    n = s[0]
    rho = WEIGHT * n
    u = [HALF * s[i + 1] / n for i in range(3)]
    h2 = HALF * HALF
    mom = [h2 * s[4 + i] for i in range(6)]
    xx, yy, zz, xy, xz, yz = mom
    energy = xx + yy + zz
    usq = u[0] * u[0] + u[1] * u[1] + u[2] * u[2]
    temp = (energy / n - usq) / 3.0
    second = [[xx, xy, xz], [xy, yy, yz], [xz, yz, zz]]
    q = []
    for i in range(3):
        third = h2 * HALF * s[10 + i]
        mixed = u[0] * second[i][0] + u[1] * second[i][1] + u[2] * second[i][2]
        q.append(0.5 * WEIGHT * (third - 2.0 * mixed - u[i] * energy + 2.0 * n * u[i] * usq))
    keep = jnp.exp(-DT * rho * jnp.sqrt(temp) / kn)
    inv = 1.0 / temp
    tau = 2.0 * math.pi * temp
    front = rho / (tau * jnp.sqrt(tau)) * (1.0 - keep)
    kappa = (1.0 / 3.0) / (5.0 * rho * temp * temp)
    b = usq * inv - 5.0
    uq = u[0] * q[0] + u[1] * q[1] + u[2] * q[2]
    fk = front * kappa
    wall, inflow = kind == 1, kind == 2
    gas = jnp.logical_not(jnp.logical_or(wall, inflow))
    zero = jnp.zeros_like(n)

    def pick(g, w, i):
        return jnp.where(wall, w, jnp.where(inflow, i, g))

    norm = (2.0 * math.pi) ** -1.5
    arg_sq = pick(-0.5 * h2 * inv, zero - 0.5 * h2, zero - 0.5 * h2)
    arg = [
        pick(-0.5 * usq * inv, zero, zero - 0.125),
        pick(HALF * u[0] * inv, zero, zero + 0.5 * HALF),
        pick(HALF * u[1] * inv, zero, zero),
        pick(HALF * u[2] * inv, zero, zero),
    ] + [arg_sq] * 3 + [zero] * 9
    poly = [pick(front - fk * uq * b, rho * norm, zero + 12.0 * norm)]
    rest = [fk * HALF * (b * q[i] + 2.0 * uq * u[i] * inv) for i in range(3)]
    rest += [-fk * h2 * inv * (2.0 * q[i] * u[i] + uq) for i in range(3)]
    rest += [
        -2.0 * fk * h2 * inv * (q[i] * u[j] + q[j] * u[i]) for i, j in ((0, 1), (0, 2), (1, 2))
    ]
    rest += [fk * h2 * HALF * inv * q[i] for i in range(3)]
    poly += [jnp.where(gas, r, 0.0) for r in rest] + [zero] * 3
    return arg, poly, jnp.where(gas, keep, 0.0)


def pieces(rows):
    whole = jnp.concatenate(rows, axis=0)
    both = jnp.concatenate([whole, whole], axis=0)
    first = both.astype(BF16).astype(F32)
    left = both - first
    second = left.astype(BF16).astype(F32)
    third = left - second
    full = jnp.concatenate([first, second, third, jnp.zeros_like(first)], axis=0)
    return full.T.astype(BF16)


def minmod_pair(mid, a, b):
    lo, hi = jnp.minimum(mid, 0.0), jnp.maximum(mid, 0.0)
    return jnp.minimum(jnp.maximum(a, lo), hi) - jnp.minimum(jnp.maximum(b, lo), hi)


def upwind(pos, far_lo, lo, mid, hi, far_hi):
    before = jnp.where(pos, lo, hi)
    after = jnp.where(pos, hi, lo)
    far = jnp.where(pos, far_lo, far_hi)
    step = mid - before
    return step + 0.5 * minmod_pair(step, after - mid, before - far)


def kernel(
    sizes, group, dist, phi_ref, lane_ref, kind_ref, kn_ref, out,
    f, g, c_send, y_send, xh, yh, acc, arg_c, poly_c, keep_c, ps,
    in_sem, out_sem, send_sem, recv_sem, ps_send, ps_recv,
):
    nsx, nsy, nvel = sizes
    ncol, nx, ny = f.shape[:3]
    cells = nx * ny
    groups = ncol // group
    x_size, y_size, v_size = nsx, nsy, nvel
    ix, iy, iv = lax.axis_index("sx"), lax.axis_index("sy"), lax.axis_index("vel")
    x_up, x_down = lax.rem(ix + 1, x_size), lax.rem(ix + x_size - 1, x_size)
    y_up, y_down = lax.rem(iy + 1, y_size), lax.rem(iy + y_size - 1, y_size)

    def in_copy(j):
        return pltpu.make_async_copy(
            dist.at[:, :, pl.ds(pl.multiple_of(j * LANES, LANES), LANES)],
            f.at[j],
            in_sem.at[j],
        )

    def out_copy(j):
        return pltpu.make_async_copy(
            f.at[j],
            out.at[:, :, pl.ds(pl.multiple_of(j * LANES, LANES), LANES)],
            out_sem.at[j],
        )

    @pl.loop(0, ncol)
    def _(j):
        in_copy(j).start()

    partners = [{"vel": lax.rem(iv + o, v_size)} for o in range(1, nvel)]
    partners += [{"sx": x_up}] + ([{"sx": x_down}] if nsx > 2 else [])
    partners += [{"sy": y_up}] + ([{"sy": y_down}] if nsy > 2 else [])
    barrier = pltpu.get_barrier_semaphore()
    for who in partners:
        pl.semaphore_signal(barrier, inc=1, device_id=who, device_id_type=MESH)
    pl.semaphore_wait(barrier, len(partners))

    def face(slab):
        return pl.ds(slab * PITCH + TOP, ny)

    def halo_copies(step, k):
        cols = pl.ds(k * group, group)

        def remote(n, src, dst, who):
            return pltpu.make_async_remote_copy(
                src_ref=src, dst_ref=dst,
                send_sem=send_sem.at[step, k, n], recv_sem=recv_sem.at[step, k, n],
                device_id=who, device_id_type=MESH,
            )

        copies = [
            remote(0, g.at[cols, face(nx + 1)], xh.at[step, cols, 1], {"sx": x_up}),
            remote(1, g.at[cols, face(2)], xh.at[step, cols, 2], {"sx": x_down}),
            remote(2, c_send.at[cols], xh.at[step, cols, 0], {"sx": x_up}),
            remote(3, y_send.at[cols, 1], yh.at[step, cols, 0], {"sy": y_up}),
            remote(4, y_send.at[cols, 0], yh.at[step, cols, 1], {"sy": y_down}),
        ]
        if nsx > 2:
            copies.append(remote(5, c_send.at[cols], xh.at[step, cols, 3], {"sx": x_down}))
        return copies

    def add_moments(j):
        phi = phi_ref[j]
        wide = jnp.concatenate([phi, phi, phi, phi], axis=0)
        both = jnp.concatenate([wide, wide], axis=1)
        for r in range(0, cells, 128):
            val = f[j, r // ny : (r + 128) // ny].reshape(128, LANES)
            hi = val.astype(BF16)
            lo = (val - hi.astype(F32)).astype(BF16)
            acc[r : r + 128, :] += lax.dot_general(
                jnp.concatenate([hi, lo], axis=1), both,
                (((1,), (1,)), ((), ())), preferred_element_type=F32,
            )

    def exchange(step):
        local = acc[...].T
        ps[step, iv] = local[0:16] + local[16:32]
        copies = []
        for o in range(1, nvel):
            copy = pltpu.make_async_remote_copy(
                src_ref=ps.at[step, iv], dst_ref=ps.at[step, iv],
                send_sem=ps_send.at[step, o], recv_sem=ps_recv.at[step, o],
                device_id={"vel": lax.rem(iv + o, v_size)}, device_id_type=MESH,
            )
            copy.start()
            copies.append(copy)
        for copy in copies:
            copy.wait()
        total = ps[step, 0]
        for v in range(1, nvel):
            total = total + ps[step, v]
        rows = [total[i : i + 1] for i in range(13)]
        arg, poly, keep = coefficients(rows, kind_ref[...], kn_ref[...])
        arg_c[...] = pieces(arg)
        poly_c[...] = pieces(poly)
        keep_c[...] = jnp.broadcast_to(keep, (LANES, cells)).T

    def relax(j):
        phi = phi_ref[j]
        wide = jnp.concatenate([phi, phi, phi, phi], axis=0)
        for r in range(0, cells, 128):
            rows = pl.ds(r, 128)
            arg = jnp.dot(arg_c[rows, :], wide, preferred_element_type=F32)
            poly = jnp.dot(poly_c[rows, :], wide, preferred_element_type=F32)
            val = f[j, r // ny : (r + 128) // ny].reshape(128, LANES)
            new = val * keep_c[rows, :] + jnp.exp(arg) * poly
            for i in range(128 // ny):
                slab = r // ny + i + 2
                g[j, face(slab), :] = new[i * ny : (i + 1) * ny]
        pos = jnp.broadcast_to(lane_ref[j, 0:1, :], (ny, LANES)) > 0.0
        c_send[j] = jnp.where(pos, g[j, face(nx), :], g[j, face(3), :])
        for side, first in ((0, 0), (1, ny - 2)):
            for layer in range(2):
                y_send[j, side, layer * nx : (layer + 1) * nx, :] = g[
                    j, pl.ds(2 * PITCH + TOP + first + layer, nx, stride=PITCH), :
                ]

    def transport(step, j):
        lanes = lane_ref[j]
        pos_x = jnp.broadcast_to(lanes[0:1], (ny, LANES)) > 0.0
        pos_y = jnp.broadcast_to(lanes[1:2], (ny, LANES)) > 0.0
        rate_x = jnp.broadcast_to(lanes[2:3], (ny, LANES))
        rate_y = jnp.broadcast_to(lanes[3:4], (ny, LANES))
        far = xh[step, j, 0]
        g[j, face(0), :] = far
        g[j, face(1), :] = xh[step, j, 1]
        g[j, face(nx + 2), :] = xh[step, j, 2]
        g[j, face(nx + 3), :] = far if nsx == 2 else xh[step, j, 3]
        for side, first in ((0, -2), (1, ny)):
            for layer in range(2):
                g[j, pl.ds(2 * PITCH + TOP + first + layer, nx, stride=PITCH), :] = yh[
                    step, j, side, layer * nx : (layer + 1) * nx, :
                ]
        for x in range(nx):
            base = (x + 2) * PITCH + TOP
            mid = g[j, pl.ds(base, ny), :]
            along_x = [g[j, pl.ds(base + d * PITCH, ny), :] for d in (-2, -1, 1, 2)]
            along_y = [g[j, pl.ds(base + d, ny), :] for d in (-2, -1, 1, 2)]
            div_x = upwind(pos_x, along_x[0], along_x[1], mid, along_x[2], along_x[3])
            div_y = upwind(pos_y, along_y[0], along_y[1], mid, along_y[2], along_y[3])
            f[j, x] = mid - (rate_x * div_x + rate_y * div_y)

    acc[...] = jnp.zeros_like(acc)

    @pl.loop(0, ncol)
    def _(j):
        in_copy(j).wait()
        add_moments(j)

    for step in range(STEPS):
        last = step == STEPS - 1
        exchange(step)

        @pl.loop(0, groups)
        def _(k):
            @pl.loop(0, group)
            def _(i):
                relax(k * group + i)

            for copy in halo_copies(step, k):
                copy.start()

        if not last:
            acc[...] = jnp.zeros_like(acc)

        @pl.loop(0, groups)
        def _(k):
            for copy in halo_copies(step, k):
                copy.wait()

            @pl.loop(0, group)
            def _(i):
                j = k * group + i
                transport(step, j)
                if last:
                    out_copy(j).start()
                else:
                    add_moments(j)

    @pl.loop(0, ncol)
    def _(j):
        out_copy(j).wait()


def body(sizes, distribution, cell_kind, local_knudsen):
    nx, ny, count = distribution.shape
    ncol = -(-count // LANES)
    width = ncol * LANES
    offset = jnp.arange(width, dtype=jnp.int32).reshape(ncol, LANES)
    phi, lane = tables(lax.axis_index("vel") * count + offset, offset < count)
    padded = distribution
    if width != count:
        padded = jnp.pad(distribution, ((0, 0), (0, 0), (0, width - count)))
    group = 3 if ncol % 3 == 0 else 1
    groups, cells = ncol // group, nx * ny
    nsx, nsy, nvel = sizes
    xcopies = 3 if nsx == 2 else 4
    dma = pltpu.SemaphoreType.DMA
    any_spec = pl.BlockSpec(memory_space=pl.ANY)
    vmem = pl.BlockSpec(memory_space=pltpu.VMEM)
    result = pl.pallas_call(
        functools.partial(kernel, sizes, group),
        out_shape=jax.ShapeDtypeStruct((nx, ny, width), F32),
        in_specs=[any_spec, vmem, vmem, vmem, vmem],
        out_specs=any_spec,
        scratch_shapes=[
            pltpu.VMEM((ncol, nx, ny, LANES), F32),
            pltpu.VMEM((ncol, (nx + 4) * PITCH, LANES), F32),
            pltpu.VMEM((ncol, ny, LANES), F32),
            pltpu.VMEM((ncol, 2, 2 * nx, LANES), F32),
            pltpu.VMEM((STEPS, ncol, xcopies, ny, LANES), F32),
            pltpu.VMEM((STEPS, ncol, 2, 2 * nx, LANES), F32),
            pltpu.VMEM((cells, LANES), F32),
            pltpu.VMEM((cells, LANES), BF16),
            pltpu.VMEM((cells, LANES), BF16),
            pltpu.VMEM((cells, LANES), F32),
            pltpu.VMEM((STEPS, nvel, 16, cells), F32),
            dma((ncol,)),
            dma((ncol,)),
            dma((STEPS, groups, xcopies + 2)),
            dma((STEPS, groups, xcopies + 2)),
            dma((STEPS, nvel)),
            dma((STEPS, nvel)),
        ],
        compiler_params=pltpu.CompilerParams(
            collective_id=0, has_side_effects=True, vmem_limit_bytes=56 * 2**20
        ),
    )(padded, phi, lane, cell_kind.reshape(1, cells), local_knudsen.reshape(1, cells))
    return result[..., :count] if width != count else result


def solution(mesh):
    sizes = (mesh.shape["sx"], mesh.shape["sy"], mesh.shape["vel"])
    return jax.shard_map(
        functools.partial(body, sizes),
        mesh=mesh,
        in_specs=(P("sx", "sy", "vel"), P("sx", "sy"), P("sx", "sy")),
        out_specs=P("sx", "sy", "vel"),
        check_vma=False,
    )
```

```python
import functools
import math

import jax
import jax.numpy as jnp
from jax import lax
from jax.experimental import pallas as pl
from jax.experimental.pallas import tpu as pltpu
from jax.sharding import PartitionSpec as P

NVX = 24
STEPS = 2
VEL_LIMIT = 4.8
DT = 0.09
SPACING = 2.0 * VEL_LIMIT / NVX
HALF = 0.5 * SPACING
WEIGHT = SPACING**3
LANES = 128
PITCH = 48
TOP = 8
MESH = pl.DeviceIdType.MESH
F32 = jnp.float32
BF16 = jnp.bfloat16


def tables(index, valid):
    plane = jnp.floor((index + 0.5) * (1.0 / NVX))
    c = jnp.floor((plane + 0.5) * (1.0 / NVX))
    m = []
    for p in (index - NVX * plane, plane - NVX * c, c):
        pair = jnp.floor(0.5 * p)
        m.append((2.0 * pair + 1.0) * (2.0 * (p - 2.0 * pair) - 1.0))
    x, y, z = m
    sq = x * x + y * y + z * z
    quads = [x * x, y * y, z * z, x * y, x * z, y * z]
    cubes = [x * sq, y * sq, z * sq]
    q_hi = [16.0 * jnp.floor((v + 8.0) * 0.0625) for v in quads]
    c_hi = [256.0 * jnp.floor((v + 128.0) * 0.00390625) for v in cubes]
    q_lo = [a - b for a, b in zip(quads, q_hi)]
    c_lo = [a - b for a, b in zip(cubes, c_hi)]
    one, zero = jnp.ones_like(x), jnp.zeros_like(x)
    rows = [one, x, y, z] + q_hi + c_hi + [zero] * 3 + [zero] * 4 + q_lo + c_lo + [zero] * 3
    phi = jnp.concatenate([jnp.where(valid, r, 0.0) for r in rows], axis=0).astype(BF16)
    speeds = [x, y, DT * HALF * jnp.abs(x), DT * HALF * jnp.abs(y)]
    return phi, jnp.concatenate(speeds + [zero] * 4, axis=0)


def coefficients(s):
    n, kind, kn = s[0], s[13], s[14]
    rho = WEIGHT * n
    u = [HALF * s[i + 1] / n for i in range(3)]
    h2 = HALF * HALF
    mom = [h2 * s[4 + i] for i in range(6)]
    xx, yy, zz, xy, xz, yz = mom
    energy = xx + yy + zz
    usq = u[0] * u[0] + u[1] * u[1] + u[2] * u[2]
    temp = (energy / n - usq) / 3.0
    second = [[xx, xy, xz], [xy, yy, yz], [xz, yz, zz]]
    q = []
    for i in range(3):
        third = h2 * HALF * s[10 + i]
        mixed = u[0] * second[i][0] + u[1] * second[i][1] + u[2] * second[i][2]
        q.append(0.5 * WEIGHT * (third - 2.0 * mixed - u[i] * energy + 2.0 * n * u[i] * usq))
    keep = jnp.exp(-DT * rho * jnp.sqrt(temp) / kn)
    inv = 1.0 / temp
    tau = 2.0 * math.pi * temp
    front = rho / (tau * jnp.sqrt(tau)) * (1.0 - keep)
    kappa = (1.0 / 3.0) / (5.0 * rho * temp * temp)
    b = usq * inv - 5.0
    uq = u[0] * q[0] + u[1] * q[1] + u[2] * q[2]
    fk = front * kappa
    wall, inflow = kind == 1.0, kind == 2.0
    gas = jnp.logical_not(jnp.logical_or(wall, inflow))
    zero = jnp.zeros_like(n)

    def pick(g, w, i):
        return jnp.where(wall, w, jnp.where(inflow, i, g))

    norm = (2.0 * math.pi) ** -1.5
    arg_sq = pick(-0.5 * h2 * inv, zero - 0.5 * h2, zero - 0.5 * h2)
    arg = [
        pick(-0.5 * usq * inv, zero, zero - 0.125),
        pick(HALF * u[0] * inv, zero, zero + 0.5 * HALF),
        pick(HALF * u[1] * inv, zero, zero),
        pick(HALF * u[2] * inv, zero, zero),
    ] + [arg_sq] * 3 + [zero] * 9
    poly = [pick(front - fk * uq * b, rho * norm, zero + 12.0 * norm)]
    rest = [fk * HALF * (b * q[i] + 2.0 * uq * u[i] * inv) for i in range(3)]
    rest += [-fk * h2 * inv * (2.0 * q[i] * u[i] + uq) for i in range(3)]
    rest += [
        -2.0 * fk * h2 * inv * (q[i] * u[j] + q[j] * u[i]) for i, j in ((0, 1), (0, 2), (1, 2))
    ]
    rest += [fk * h2 * HALF * inv * q[i] for i in range(3)]
    poly += [jnp.where(gas, r, 0.0) for r in rest] + [zero] * 3
    return arg, poly, jnp.where(gas, keep, 0.0)


def pieces(rows):
    whole = jnp.concatenate(rows, axis=0)
    both = jnp.concatenate([whole, whole], axis=0)
    first = both.astype(BF16).astype(F32)
    left = both - first
    second = left.astype(BF16).astype(F32)
    third = left - second
    full = jnp.concatenate([first, second, third, jnp.zeros_like(first)], axis=0)
    return full.T.astype(BF16)


def minmod_pair(mid, a, b):
    lo, hi = jnp.minimum(mid, 0.0), jnp.maximum(mid, 0.0)
    return jnp.minimum(jnp.maximum(a, lo), hi) - jnp.minimum(jnp.maximum(b, lo), hi)


def upwind(pos, far_lo, lo, mid, hi, far_hi):
    before = jnp.where(pos, lo, hi)
    after = jnp.where(pos, hi, lo)
    far = jnp.where(pos, far_lo, far_hi)
    step = mid - before
    return step + 0.5 * minmod_pair(step, after - mid, before - far)


def kernel(
    sizes, group, head, count, dist, kind_ref, kn_ref, out,
    f, g, c_send, y_send, xh, yh, acc, phi_ref, lane_ref,
    arg_c, poly_c, keep_c, arg_h, poly_h, keep_h, ps, sums, y_sums, near,
    in_sem, out_sem, send_sem, recv_sem, ps_send, ps_recv, near_send, near_recv,
):
    nsx, nsy, nvel = sizes
    ncol, nx, ny = f.shape[:3]
    cells = nx * ny
    halo = 4 * (nx + ny)
    halo_pad = arg_h.shape[0]
    groups = ncol // group
    ix, iy, iv = lax.axis_index("sx"), lax.axis_index("sy"), lax.axis_index("vel")
    x_up, x_down = lax.rem(ix + 1, nsx), lax.rem(ix + nsx - 1, nsx)
    y_up, y_down = lax.rem(iy + 1, nsy), lax.rem(iy + nsy - 1, nsy)

    def lanes_of(ref, j):
        return ref.at[:, :, pl.ds(pl.multiple_of(j * LANES, LANES), LANES)]

    def in_copy(j):
        return pltpu.make_async_copy(lanes_of(dist, j), f.at[j], in_sem.at[j])

    def out_copy(j):
        return pltpu.make_async_copy(f.at[j], lanes_of(out, j), out_sem.at[j])

    @pl.loop(0, ncol)
    def _(j):
        in_copy(j).start()

    partners = [{"vel": lax.rem(iv + o, nvel)} for o in range(1, nvel)]
    partners += [{"sx": x_up}] + ([{"sx": x_down}] if nsx > 2 else [])
    partners += [{"sy": y_up}] + ([{"sy": y_down}] if nsy > 2 else [])
    barrier = pltpu.get_barrier_semaphore()
    for who in partners:
        pl.semaphore_signal(barrier, inc=1, device_id=who, device_id_type=MESH)

    @pl.loop(0, ncol)
    def _(j):
        offset = j * LANES + lax.broadcasted_iota(jnp.int32, (1, LANES), 1)
        phi, lane_ref[j] = tables((iv * count + offset).astype(F32), offset < count)
        phi_ref[j] = jnp.concatenate([phi] * 4, axis=0)

    kind = kind_ref[...].astype(F32)
    kn = kn_ref[...]
    kind_row = jnp.concatenate([kind[x : x + 1] for x in range(nx)], axis=1)
    kn_row = jnp.concatenate([kn[x : x + 1] for x in range(nx)], axis=1)
    acc[...] = jnp.zeros_like(acc)
    pl.semaphore_wait(barrier, len(partners))

    def face(slab):
        return pl.ds(slab * PITCH + TOP, ny)

    def halo_copies(step, k):
        cols = pl.ds(k * group, group)

        def remote(n, src, dst, who):
            return pltpu.make_async_remote_copy(
                src_ref=src, dst_ref=dst,
                send_sem=send_sem.at[step, k, n], recv_sem=recv_sem.at[step, k, n],
                device_id=who, device_id_type=MESH,
            )

        copies = [
            remote(0, f.at[cols, nx - 1], xh.at[step, cols, 1], {"sx": x_up}),
            remote(1, f.at[cols, 0], xh.at[step, cols, 2], {"sx": x_down}),
            remote(2, c_send.at[cols], xh.at[step, cols, 0], {"sx": x_up}),
            remote(3, y_send.at[cols, 1], yh.at[step, cols, 0], {"sy": y_up}),
            remote(4, y_send.at[cols, 0], yh.at[step, cols, 1], {"sy": y_down}),
        ]
        if nsx > 2:
            copies.append(remote(5, c_send.at[cols], xh.at[step, cols, 3], {"sx": x_down}))
        return copies

    def near_copies(step):
        edge = 4 * ny

        def remote(n, src, first, rows, who):
            return pltpu.make_async_remote_copy(
                src_ref=src, dst_ref=near.at[step, pl.ds(first, rows)],
                send_sem=near_send.at[step, n], recv_sem=near_recv.at[step, n],
                device_id=who, device_id_type=MESH,
            )

        return [
            remote(0, sums.at[step, pl.ds(cells - 2 * ny, 2 * ny)], 0, 2 * ny, {"sx": x_up}),
            remote(1, sums.at[step, pl.ds(0, 2 * ny)], 2 * ny, 2 * ny, {"sx": x_down}),
            remote(2, y_sums.at[step, 1], edge, 2 * nx, {"sy": y_up}),
            remote(3, y_sums.at[step, 0], edge + 2 * nx, 2 * nx, {"sy": y_down}),
        ]

    def pack(j):
        pos = jnp.broadcast_to(lane_ref[j, 0:1, :], (ny, LANES)) > 0.0
        c_send[j] = jnp.where(pos, f[j, nx - 2], f[j, 1])
        for side, first in ((0, 0), (1, ny - 2)):
            for layer in range(2):
                y_send[j, side, layer * nx : (layer + 1) * nx, :] = f[j, :, first + layer, :]

    def add_moments(j):
        wide = phi_ref[j]
        both = jnp.concatenate([wide, wide], axis=1)
        for r in range(0, cells, 128):
            val = f[j, r // ny : (r + 128) // ny].reshape(128, LANES)
            hi = val.astype(BF16)
            lo = (val - hi.astype(F32)).astype(BF16)
            acc[r : r + 128, :] += lax.dot_general(
                jnp.concatenate([hi, lo], axis=1), both,
                (((1,), (1,)), ((), ())), preferred_element_type=F32,
            )

    def exchange(step):
        local = acc[...].T
        ps[step, iv] = local[0:16] + local[16:32]
        copies = []
        for o in range(1, nvel):
            copy = pltpu.make_async_remote_copy(
                src_ref=ps.at[step, iv], dst_ref=ps.at[step, iv],
                send_sem=ps_send.at[step, o], recv_sem=ps_recv.at[step, o],
                device_id={"vel": lax.rem(iv + o, nvel)}, device_id_type=MESH,
            )
            copy.start()
            copies.append(copy)
        for copy in copies:
            copy.wait()
        total = ps[step, 0]
        for v in range(1, nvel):
            total = total + ps[step, v]
        blank = jnp.zeros((113, cells), F32)
        total = jnp.concatenate([total[0:13], kind_row, kn_row, blank], axis=0)
        sums[step] = total.T
        for side, first in ((0, 0), (1, ny - 2)):
            for layer in range(2):
                y_sums[step, side, layer * nx : (layer + 1) * nx, :] = sums[
                    step, pl.ds(first + layer, nx, stride=ny), :
                ]
        for copy in near_copies(step):
            copy.start()
        return total

    def set_coefficients(total, arg_ref, poly_ref, keep_ref):
        arg, poly, keep = coefficients([total[i : i + 1] for i in range(15)])
        arg_ref[...] = pieces(arg)
        poly_ref[...] = pieces(poly)
        keep_ref[...] = jnp.broadcast_to(keep, (LANES, keep.shape[1])).T

    def relax(j):
        wide = phi_ref[j]
        for r in range(0, cells, 128):
            rows = pl.ds(r, 128)
            arg = jnp.dot(arg_c[rows, :], wide, preferred_element_type=F32)
            poly = jnp.dot(poly_c[rows, :], wide, preferred_element_type=F32)
            val = f[j, r // ny : (r + 128) // ny].reshape(128, LANES)
            new = val * keep_c[rows, :] + jnp.exp(arg) * poly
            for i in range(128 // ny):
                g[j, face(r // ny + i + 2), :] = new[i * ny : (i + 1) * ny]

    def relax_halo(step, j):
        wide = phi_ref[j]
        rows = pl.ds(0, halo)
        arg = jnp.dot(arg_h[rows, :], wide, preferred_element_type=F32)
        poly = jnp.dot(poly_h[rows, :], wide, preferred_element_type=F32)
        far_lo = xh[step, j, 0]
        far_hi = far_lo if nsx == 2 else xh[step, j, 3]
        val = jnp.concatenate(
            [far_lo, xh[step, j, 1], xh[step, j, 2], far_hi, yh[step, j, 0], yh[step, j, 1]], axis=0
        )
        new = val * keep_h[rows, :] + jnp.exp(arg) * poly
        for i, slab in enumerate((0, 1, nx + 2, nx + 3)):
            g[j, face(slab), :] = new[i * ny : (i + 1) * ny]
        for i, first in enumerate((-2, -1, ny, ny + 1)):
            at = 4 * ny + i * nx
            g[j, pl.ds(2 * PITCH + TOP + first, nx, stride=PITCH), :] = new[at : at + nx]

    def transport(j):
        lanes = lane_ref[j]
        pos_x = jnp.broadcast_to(lanes[0:1], (ny, LANES)) > 0.0
        pos_y = jnp.broadcast_to(lanes[1:2], (ny, LANES)) > 0.0
        rate_x = jnp.broadcast_to(lanes[2:3], (ny, LANES))
        rate_y = jnp.broadcast_to(lanes[3:4], (ny, LANES))
        for x in range(nx):
            base = (x + 2) * PITCH + TOP
            mid = g[j, pl.ds(base, ny), :]
            along_x = [g[j, pl.ds(base + d * PITCH, ny), :] for d in (-2, -1, 1, 2)]
            along_y = [g[j, pl.ds(base + d, ny), :] for d in (-2, -1, 1, 2)]
            div_x = upwind(pos_x, along_x[0], along_x[1], mid, along_x[2], along_x[3])
            div_y = upwind(pos_y, along_y[0], along_y[1], mid, along_y[2], along_y[3])
            f[j, x] = mid - (rate_x * div_x + rate_y * div_y)

    def send(step, k):
        for copy in halo_copies(step, k):
            copy.start()

    @pl.loop(0, groups)
    def _(k):
        @pl.loop(0, group)
        def _(i):
            j = k * group + i
            in_copy(j).wait()
            pack(j)
            add_moments(j)

        @pl.when(k < head)
        def _():
            send(0, k)

    for step in range(STEPS):
        last = step == STEPS - 1
        total = exchange(step)

        @pl.loop(head, groups)
        def _(k):
            send(step, k)

        set_coefficients(total, arg_c, poly_c, keep_c)

        @pl.loop(0, ncol)
        def _(j):
            relax(j)

        for copy in near_copies(step):
            copy.wait()
        around = [near[step, 0:halo, :]]
        if halo_pad > halo:
            around.append(sums[step, 0 : halo_pad - halo, :])
        set_coefficients(jnp.concatenate(around, axis=0).T, arg_h, poly_h, keep_h)
        if not last:
            acc[...] = jnp.zeros_like(acc)

        @pl.loop(0, groups)
        def _(k):
            for copy in halo_copies(step, k):
                copy.wait()

            @pl.loop(0, group)
            def _(i):
                j = k * group + i
                relax_halo(step, j)
                transport(j)
                if last:
                    out_copy(j).start()
                else:
                    pack(j)
                    add_moments(j)

            if not last:
                @pl.when(k < head)
                def _():
                    send(step + 1, k)

    @pl.loop(0, ncol)
    def _(j):
        out_copy(j).wait()


def body(sizes, distribution, cell_kind, local_knudsen):
    nx, ny, count = distribution.shape
    ncol = -(-count // LANES)
    width = ncol * LANES
    padded = distribution
    if width != count:
        padded = jnp.pad(distribution, ((0, 0), (0, 0), (0, width - count)))
    group = 3 if ncol % 3 == 0 else 1
    groups, cells = ncol // group, nx * ny
    halo_pad = -(-4 * (nx + ny) // LANES) * LANES
    head = (4 * groups + 8) // 9
    nsx, nsy, nvel = sizes
    xcopies = 3 if nsx == 2 else 4
    dma = pltpu.SemaphoreType.DMA
    vmem = pl.BlockSpec(memory_space=pltpu.VMEM)
    result = pl.pallas_call(
        functools.partial(kernel, sizes, group, head, count),
        out_shape=jax.ShapeDtypeStruct((nx, ny, width), F32),
        in_specs=[pl.BlockSpec(memory_space=pltpu.MemorySpace.HBM), vmem, vmem],
        out_specs=pl.BlockSpec(memory_space=pl.ANY),
        scratch_shapes=[
            pltpu.VMEM((ncol, nx, ny, LANES), F32),
            pltpu.VMEM((ncol, (nx + 4) * PITCH, LANES), F32),
            pltpu.VMEM((ncol, ny, LANES), F32),
            pltpu.VMEM((ncol, 2, 2 * nx, LANES), F32),
            pltpu.VMEM((STEPS, ncol, xcopies, ny, LANES), F32),
            pltpu.VMEM((STEPS, ncol, 2, 2 * nx, LANES), F32),
            pltpu.VMEM((cells, LANES), F32),
            pltpu.VMEM((ncol, LANES, LANES), BF16),
            pltpu.VMEM((ncol, 8, LANES), F32),
            pltpu.VMEM((cells, LANES), BF16),
            pltpu.VMEM((cells, LANES), BF16),
            pltpu.VMEM((cells, LANES), F32),
            pltpu.VMEM((halo_pad, LANES), BF16),
            pltpu.VMEM((halo_pad, LANES), BF16),
            pltpu.VMEM((halo_pad, LANES), F32),
            pltpu.VMEM((STEPS, nvel, 16, cells), F32),
            pltpu.VMEM((STEPS, cells, LANES), F32),
            pltpu.VMEM((STEPS, 2, 2 * nx, LANES), F32),
            pltpu.VMEM((STEPS, 4 * (nx + ny), LANES), F32),
            dma((ncol,)),
            dma((ncol,)),
            dma((STEPS, groups, xcopies + 2)),
            dma((STEPS, groups, xcopies + 2)),
            dma((STEPS, nvel)),
            dma((STEPS, nvel)),
            dma((STEPS, 4)),
            dma((STEPS, 4)),
        ],
        compiler_params=pltpu.CompilerParams(
            collective_id=0, has_side_effects=True, vmem_limit_bytes=40 * 2**20
        ),
    )(padded, cell_kind, local_knudsen)
    return result[..., :count] if width != count else result


def solution(mesh):
    sizes = (mesh.shape["sx"], mesh.shape["sy"], mesh.shape["vel"])
    return jax.shard_map(
        functools.partial(body, sizes),
        mesh=mesh,
        in_specs=(P("sx", "sy", "vel"), P("sx", "sy"), P("sx", "sy")),
        out_specs=P("sx", "sy", "vel"),
        check_vma=False,
    )
```

```python
import functools
import math

import jax
import jax.numpy as jnp
from jax import lax
from jax.experimental import pallas as pl
from jax.experimental.pallas import tpu as pltpu
from jax.sharding import PartitionSpec as P

NVX = 24
STEPS = 2
VEL_LIMIT = 4.8
DT = 0.09
SPACING = 2.0 * VEL_LIMIT / NVX
HALF = 0.5 * SPACING
WEIGHT = SPACING**3
LANES = 128
PITCH = 48
TOP = 8
MESH = pl.DeviceIdType.MESH
F32 = jnp.float32
BF16 = jnp.bfloat16


def tables(index, valid):
    plane = jnp.floor((index + 0.5) * (1.0 / NVX))
    c = jnp.floor((plane + 0.5) * (1.0 / NVX))
    m = []
    for p in (index - NVX * plane, plane - NVX * c, c):
        pair = jnp.floor(0.5 * p)
        m.append((2.0 * pair + 1.0) * (2.0 * (p - 2.0 * pair) - 1.0))
    x, y, z = m
    sq = x * x + y * y + z * z
    quads = [x * x, y * y, z * z, x * y, x * z, y * z]
    cubes = [x * sq, y * sq, z * sq]
    q_hi = [16.0 * jnp.floor((v + 8.0) * 0.0625) for v in quads]
    c_hi = [256.0 * jnp.floor((v + 128.0) * 0.00390625) for v in cubes]
    q_lo = [a - b for a, b in zip(quads, q_hi)]
    c_lo = [a - b for a, b in zip(cubes, c_hi)]
    one, zero = jnp.ones_like(x), jnp.zeros_like(x)
    rows = [one, x, y, z] + q_hi + c_hi + [zero] * 3 + [zero] * 4 + q_lo + c_lo + [zero] * 3
    phi = jnp.concatenate([jnp.where(valid, r, 0.0) for r in rows], axis=0).astype(BF16)
    speeds = [x, y, DT * HALF * x, DT * HALF * jnp.abs(y)]
    return phi, jnp.concatenate(speeds + [zero] * 4, axis=0)


def coefficients(s):
    n, kind, kn = s[0], s[13], s[14]
    rho = WEIGHT * n
    u = [HALF * s[i + 1] / n for i in range(3)]
    h2 = HALF * HALF
    mom = [h2 * s[4 + i] for i in range(6)]
    xx, yy, zz, xy, xz, yz = mom
    energy = xx + yy + zz
    usq = u[0] * u[0] + u[1] * u[1] + u[2] * u[2]
    temp = (energy / n - usq) / 3.0
    second = [[xx, xy, xz], [xy, yy, yz], [xz, yz, zz]]
    q = []
    for i in range(3):
        third = h2 * HALF * s[10 + i]
        mixed = u[0] * second[i][0] + u[1] * second[i][1] + u[2] * second[i][2]
        q.append(0.5 * WEIGHT * (third - 2.0 * mixed - u[i] * energy + 2.0 * n * u[i] * usq))
    keep = jnp.exp(-DT * rho * jnp.sqrt(temp) / kn)
    inv = 1.0 / temp
    tau = 2.0 * math.pi * temp
    front = rho / (tau * jnp.sqrt(tau)) * (1.0 - keep)
    kappa = (1.0 / 3.0) / (5.0 * rho * temp * temp)
    b = usq * inv - 5.0
    uq = u[0] * q[0] + u[1] * q[1] + u[2] * q[2]
    fk = front * kappa
    wall, inflow = kind == 1.0, kind == 2.0
    gas = jnp.logical_not(jnp.logical_or(wall, inflow))
    zero = jnp.zeros_like(n)

    def pick(g, w, i):
        return jnp.where(wall, w, jnp.where(inflow, i, g))

    norm = (2.0 * math.pi) ** -1.5
    arg_sq = pick(-0.5 * h2 * inv, zero - 0.5 * h2, zero - 0.5 * h2)
    arg = [
        pick(-0.5 * usq * inv, zero, zero - 0.125),
        pick(HALF * u[0] * inv, zero, zero + 0.5 * HALF),
        pick(HALF * u[1] * inv, zero, zero),
        pick(HALF * u[2] * inv, zero, zero),
    ] + [arg_sq] * 3 + [zero] * 9
    poly = [pick(front - fk * uq * b, rho * norm, zero + 12.0 * norm)]
    rest = [fk * HALF * (b * q[i] + 2.0 * uq * u[i] * inv) for i in range(3)]
    rest += [-fk * h2 * inv * (2.0 * q[i] * u[i] + uq) for i in range(3)]
    rest += [
        -2.0 * fk * h2 * inv * (q[i] * u[j] + q[j] * u[i]) for i, j in ((0, 1), (0, 2), (1, 2))
    ]
    rest += [fk * h2 * HALF * inv * q[i] for i in range(3)]
    poly += [jnp.where(gas, r, 0.0) for r in rest] + [zero] * 3
    return arg, poly, jnp.where(gas, keep, 0.0)


def pieces(rows):
    whole = jnp.concatenate(rows, axis=0)
    both = jnp.concatenate([whole, whole], axis=0)
    first = both.astype(BF16).astype(F32)
    left = both - first
    second = left.astype(BF16).astype(F32)
    third = left - second
    full = jnp.concatenate([first, second, third, jnp.zeros_like(first)], axis=0)
    return full.T.astype(BF16)


def minmod_pair(mid, a, b):
    lo, hi = jnp.minimum(mid, 0.0), jnp.maximum(mid, 0.0)
    return jnp.minimum(jnp.maximum(a, lo), hi) - jnp.minimum(jnp.maximum(b, lo), hi)


def upwind(pos, far_lo, lo, mid, hi, far_hi):
    before = jnp.where(pos, lo, hi)
    after = jnp.where(pos, hi, lo)
    far = jnp.where(pos, far_lo, far_hi)
    step = mid - before
    return step + 0.5 * minmod_pair(step, after - mid, before - far)


def kernel(
    sizes, group, head, count, dist, kind_in, kn_in, out,
    kind_ref, kn_ref, f, g, c_send, y_send, xh, yh, acc, phi_ref, lane_ref,
    arg_c, poly_c, keep_c, arg_h, poly_h, keep_h, ps, sums, y_sums, near,
    cell_sem, in_sem, out_sem, send_sem, recv_sem, ps_send, ps_recv, near_send, near_recv,
):
    nsx, nsy, nvel = sizes
    ncol, nx, ny = f.shape[:3]
    cells = nx * ny
    halo = 4 * (nx + ny)
    halo_pad = arg_h.shape[0]
    groups = ncol // group
    ix, iy, iv = lax.axis_index("sx"), lax.axis_index("sy"), lax.axis_index("vel")
    x_up, x_down = lax.rem(ix + 1, nsx), lax.rem(ix + nsx - 1, nsx)
    y_up, y_down = lax.rem(iy + 1, nsy), lax.rem(iy + nsy - 1, nsy)

    def lanes_of(ref, j):
        return ref.at[:, :, pl.ds(pl.multiple_of(j * LANES, LANES), LANES)]

    def in_copy(j):
        return pltpu.make_async_copy(lanes_of(dist, j), f.at[j], in_sem.at[j])

    def out_copy(j):
        return pltpu.make_async_copy(f.at[j], lanes_of(out, j), out_sem.at[j])

    cell_copies = [
        pltpu.make_async_copy(kind_in, kind_ref, cell_sem.at[0]),
        pltpu.make_async_copy(kn_in, kn_ref, cell_sem.at[1]),
    ]

    @pl.loop(0, ncol)
    def _(j):
        in_copy(j).start()

    for copy in cell_copies:
        copy.start()

    partners = [{"vel": lax.rem(iv + o, nvel)} for o in range(1, nvel)]
    partners += [{"sx": x_up}] + ([{"sx": x_down}] if nsx > 2 else [])
    partners += [{"sy": y_up}] + ([{"sy": y_down}] if nsy > 2 else [])
    barrier = pltpu.get_barrier_semaphore()
    for who in partners:
        pl.semaphore_signal(barrier, inc=1, device_id=who, device_id_type=MESH)

    acc[...] = jnp.zeros_like(acc)
    pl.semaphore_wait(barrier, len(partners))

    def face(slab):
        return pl.ds(slab * PITCH + TOP, ny)

    def halo_copies(step, k):
        cols = pl.ds(k * group, group)

        def remote(n, src, dst, who):
            return pltpu.make_async_remote_copy(
                src_ref=src, dst_ref=dst,
                send_sem=send_sem.at[step, k, n], recv_sem=recv_sem.at[step, k, n],
                device_id=who, device_id_type=MESH,
            )

        copies = [
            remote(0, f.at[cols, nx - 1], xh.at[step, cols, 1], {"sx": x_up}),
            remote(1, f.at[cols, 0], xh.at[step, cols, 2], {"sx": x_down}),
            remote(2, c_send.at[cols], xh.at[step, cols, 0], {"sx": x_up}),
            remote(3, y_send.at[cols, 1], yh.at[step, cols, 0], {"sy": y_up}),
            remote(4, y_send.at[cols, 0], yh.at[step, cols, 1], {"sy": y_down}),
        ]
        if nsx > 2:
            copies.append(remote(5, c_send.at[cols], xh.at[step, cols, 3], {"sx": x_down}))
        return copies

    def near_copies(step):
        edge = 4 * ny

        def remote(n, src, first, rows, who):
            return pltpu.make_async_remote_copy(
                src_ref=src, dst_ref=near.at[step, pl.ds(first, rows)],
                send_sem=near_send.at[step, n], recv_sem=near_recv.at[step, n],
                device_id=who, device_id_type=MESH,
            )

        return [
            remote(0, sums.at[step, pl.ds(cells - 2 * ny, 2 * ny)], 0, 2 * ny, {"sx": x_up}),
            remote(1, sums.at[step, pl.ds(0, 2 * ny)], 2 * ny, 2 * ny, {"sx": x_down}),
            remote(2, y_sums.at[step, 1], edge, 2 * nx, {"sy": y_up}),
            remote(3, y_sums.at[step, 0], edge + 2 * nx, 2 * nx, {"sy": y_down}),
        ]

    def build_tables(j):
        offset = j * LANES + lax.broadcasted_iota(jnp.int32, (1, LANES), 1)
        phi, lane_ref[j] = tables((iv * count + offset).astype(F32), offset < count)
        phi_ref[j] = jnp.concatenate([phi] * 4, axis=0)

    def pack(j):
        pos = jnp.broadcast_to(lane_ref[j, 0:1, :], (ny, LANES)) > 0.0
        c_send[j] = jnp.where(pos, f[j, nx - 2], f[j, 1])
        for side, first in ((0, 0), (1, ny - 2)):
            for layer in range(2):
                y_send[j, side, layer * nx : (layer + 1) * nx, :] = f[j, :, first + layer, :]

    def add_moments(j):
        wide = phi_ref[j]
        both = jnp.concatenate([wide, wide], axis=1)
        for r in range(0, cells, 128):
            val = f[j, r // ny : (r + 128) // ny].reshape(128, LANES)
            hi = val.astype(BF16)
            lo = (val - hi.astype(F32)).astype(BF16)
            acc[r : r + 128, :] += lax.dot_general(
                jnp.concatenate([hi, lo], axis=1), both,
                (((1,), (1,)), ((), ())), preferred_element_type=F32,
            )

    def exchange(step):
        local = acc[...].T
        ps[step, iv] = local[0:16] + local[16:32]
        copies = []
        for o in range(1, nvel):
            copy = pltpu.make_async_remote_copy(
                src_ref=ps.at[step, iv], dst_ref=ps.at[step, iv],
                send_sem=ps_send.at[step, o], recv_sem=ps_recv.at[step, o],
                device_id={"vel": lax.rem(iv + o, nvel)}, device_id_type=MESH,
            )
            copy.start()
            copies.append(copy)
        for copy in copies:
            copy.wait()
        total = ps[step, 0]
        for v in range(1, nvel):
            total = total + ps[step, v]
        blank = jnp.zeros((113, cells), F32)
        total = jnp.concatenate([total[0:13], kind_row, kn_row, blank], axis=0)
        sums[step] = total.T
        for side, first in ((0, 0), (1, ny - 2)):
            for layer in range(2):
                y_sums[step, side, layer * nx : (layer + 1) * nx, :] = sums[
                    step, pl.ds(first + layer, nx, stride=ny), :
                ]
        for copy in near_copies(step):
            copy.start()
        return total

    def set_coefficients(total, arg_ref, poly_ref, keep_ref):
        arg, poly, keep = coefficients([total[i : i + 1] for i in range(15)])
        arg_ref[...] = pieces(arg)
        poly_ref[...] = pieces(poly)
        keep_ref[...] = jnp.broadcast_to(keep, (LANES, keep.shape[1])).T

    def relax(j):
        wide = phi_ref[j]
        for r in range(0, cells, 128):
            rows = pl.ds(r, 128)
            arg = jnp.dot(arg_c[rows, :], wide, preferred_element_type=F32)
            poly = jnp.dot(poly_c[rows, :], wide, preferred_element_type=F32)
            val = f[j, r // ny : (r + 128) // ny].reshape(128, LANES)
            new = val * keep_c[rows, :] + jnp.exp(arg) * poly
            for i in range(128 // ny):
                g[j, face(r // ny + i + 2), :] = new[i * ny : (i + 1) * ny]

    def relax_halo(step, j):
        wide = phi_ref[j]
        rows = pl.ds(0, halo)
        arg = jnp.dot(arg_h[rows, :], wide, preferred_element_type=F32)
        poly = jnp.dot(poly_h[rows, :], wide, preferred_element_type=F32)
        far_lo = xh[step, j, 0]
        far_hi = far_lo if nsx == 2 else xh[step, j, 3]
        val = jnp.concatenate(
            [far_lo, xh[step, j, 1], xh[step, j, 2], far_hi, yh[step, j, 0], yh[step, j, 1]], axis=0
        )
        new = val * keep_h[rows, :] + jnp.exp(arg) * poly
        for i, slab in enumerate((0, 1, nx + 2, nx + 3)):
            g[j, face(slab), :] = new[i * ny : (i + 1) * ny]
        for i, first in enumerate((-2, -1, ny, ny + 1)):
            at = 4 * ny + i * nx
            g[j, pl.ds(2 * PITCH + TOP + first, nx, stride=PITCH), :] = new[at : at + nx]

    def transport(j):
        half = ny // 2
        lanes = [jnp.broadcast_to(lane_ref[j, i : i + 1, :], (half, LANES)) for i in range(4)]
        pos_x, pos_y = lanes[0] > 0.0, lanes[1] > 0.0
        side_x = jnp.where(pos_x, 0.5, -0.5)
        rate_x, rate_y = lanes[2:]
        for row in (0, half):

            def cells_at(x, d=0):
                return g[j, pl.ds((x + 2) * PITCH + TOP + row + d, half), :]

            low, mid = cells_at(-2), cells_at(-1)
            diff = mid - low
            kept = face_value = flux = None
            for x in range(-1, nx + 1):
                high = cells_at(x + 1)
                ahead = high - mid
                slope = jnp.minimum(
                    jnp.maximum(ahead, jnp.minimum(diff, 0.0)), jnp.maximum(diff, 0.0)
                )
                value = mid + side_x * slope
                if x >= 0:
                    new_flux = jnp.where(pos_x, face_value, value)
                if x >= 1:
                    along = [cells_at(x - 1, d) for d in (-2, -1, 1, 2)]
                    div_y = upwind(pos_y, along[0], along[1], kept, along[2], along[3])
                    f[j, x - 1, row : row + half, :] = kept - (
                        rate_x * (new_flux - flux) + rate_y * div_y
                    )
                if x >= 0:
                    flux = new_flux
                kept, face_value, mid, diff = mid, value, high, ahead

    def send(step, k):
        for copy in halo_copies(step, k):
            copy.start()

    @pl.loop(0, groups)
    def _(k):
        @pl.loop(0, group)
        def _(i):
            j = k * group + i
            build_tables(j)
            in_copy(j).wait()
            pack(j)

        @pl.when(k < head)
        def _():
            send(0, k)

        @pl.loop(0, group)
        def _(i):
            add_moments(k * group + i)

    for copy in cell_copies:
        copy.wait()
    kind = kind_ref[...].astype(F32)
    kn = kn_ref[...]
    kind_row = jnp.concatenate([kind[x : x + 1] for x in range(nx)], axis=1)
    kn_row = jnp.concatenate([kn[x : x + 1] for x in range(nx)], axis=1)

    for step in range(STEPS):
        last = step == STEPS - 1
        total = exchange(step)

        @pl.loop(head, groups)
        def _(k):
            send(step, k)

        set_coefficients(total, arg_c, poly_c, keep_c)

        @pl.loop(0, ncol)
        def _(j):
            relax(j)

        for copy in near_copies(step):
            copy.wait()
        around = [near[step, 0:halo, :]]
        if halo_pad > halo:
            around.append(sums[step, 0 : halo_pad - halo, :])
        set_coefficients(jnp.concatenate(around, axis=0).T, arg_h, poly_h, keep_h)
        if not last:
            acc[...] = jnp.zeros_like(acc)

        @pl.loop(0, groups)
        def _(k):
            for copy in halo_copies(step, k):
                copy.wait()

            @pl.loop(0, group)
            def _(i):
                j = k * group + i
                relax_halo(step, j)
                transport(j)
                if last:
                    out_copy(j).start()
                else:
                    pack(j)

            if not last:
                @pl.when(k < head)
                def _():
                    send(step + 1, k)

                @pl.loop(0, group)
                def _(i):
                    add_moments(k * group + i)

    @pl.loop(0, ncol)
    def _(j):
        out_copy(j).wait()


def body(sizes, distribution, cell_kind, local_knudsen):
    nx, ny, count = distribution.shape
    ncol = -(-count // LANES)
    width = ncol * LANES
    padded = distribution
    if width != count:
        padded = jnp.pad(distribution, ((0, 0), (0, 0), (0, width - count)))
    group = 3 if ncol % 3 == 0 else 1
    groups, cells = ncol // group, nx * ny
    halo_pad = -(-4 * (nx + ny) // LANES) * LANES
    head = (4 * groups + 8) // 9
    nsx, nsy, nvel = sizes
    xcopies = 3 if nsx == 2 else 4
    dma = pltpu.SemaphoreType.DMA
    operands = [
        pltpu.with_memory_space_constraint(a, pltpu.MemorySpace.HBM)
        for a in (padded, cell_kind, local_knudsen)
    ]
    result = pl.pallas_call(
        functools.partial(kernel, sizes, group, head, count),
        out_shape=jax.ShapeDtypeStruct((nx, ny, width), F32),
        in_specs=[pl.BlockSpec(memory_space=pltpu.MemorySpace.HBM)] * 3,
        out_specs=pl.BlockSpec(memory_space=pl.ANY),
        scratch_shapes=[
            pltpu.VMEM((nx, ny), jnp.int32),
            pltpu.VMEM((nx, ny), F32),
            pltpu.VMEM((ncol, nx, ny, LANES), F32),
            pltpu.VMEM((ncol, (nx + 4) * PITCH, LANES), F32),
            pltpu.VMEM((ncol, ny, LANES), F32),
            pltpu.VMEM((ncol, 2, 2 * nx, LANES), F32),
            pltpu.VMEM((STEPS, ncol, xcopies, ny, LANES), F32),
            pltpu.VMEM((STEPS, ncol, 2, 2 * nx, LANES), F32),
            pltpu.VMEM((cells, LANES), F32),
            pltpu.VMEM((ncol, LANES, LANES), BF16),
            pltpu.VMEM((ncol, 8, LANES), F32),
            pltpu.VMEM((cells, LANES), BF16),
            pltpu.VMEM((cells, LANES), BF16),
            pltpu.VMEM((cells, LANES), F32),
            pltpu.VMEM((halo_pad, LANES), BF16),
            pltpu.VMEM((halo_pad, LANES), BF16),
            pltpu.VMEM((halo_pad, LANES), F32),
            pltpu.VMEM((STEPS, nvel, 16, cells), F32),
            pltpu.VMEM((STEPS, cells, LANES), F32),
            pltpu.VMEM((STEPS, 2, 2 * nx, LANES), F32),
            pltpu.VMEM((STEPS, 4 * (nx + ny), LANES), F32),
            dma((2,)),
            dma((ncol,)),
            dma((ncol,)),
            dma((STEPS, groups, xcopies + 2)),
            dma((STEPS, groups, xcopies + 2)),
            dma((STEPS, nvel)),
            dma((STEPS, nvel)),
            dma((STEPS, 4)),
            dma((STEPS, 4)),
        ],
        compiler_params=pltpu.CompilerParams(
            collective_id=0, has_side_effects=True, vmem_limit_bytes=40 * 2**20
        ),
    )(*operands)
    return result[..., :count] if width != count else result


def solution(mesh):
    sizes = (mesh.shape["sx"], mesh.shape["sy"], mesh.shape["vel"])
    return jax.shard_map(
        functools.partial(body, sizes),
        mesh=mesh,
        in_specs=(P("sx", "sy", "vel"), P("sx", "sy"), P("sx", "sy")),
        out_specs=P("sx", "sy", "vel"),
        check_vma=False,
    )
```

```python
import functools
import math

import jax
import jax.numpy as jnp
from jax import lax
from jax.experimental import pallas as pl
from jax.experimental.pallas import tpu as pltpu
from jax.sharding import PartitionSpec as P

NVX = 24
STEPS = 2
VEL_LIMIT = 4.8
DT = 0.09
SPACING = 2.0 * VEL_LIMIT / NVX
HALF = 0.5 * SPACING
WEIGHT = SPACING**3
LANES = 128
PITCH = 48
TOP = 8
MESH = pl.DeviceIdType.MESH
F32 = jnp.float32
BF16 = jnp.bfloat16


def tables(index, valid):
    plane = jnp.floor((index + 0.5) * (1.0 / NVX))
    c = jnp.floor((plane + 0.5) * (1.0 / NVX))
    m = []
    for p in (index - NVX * plane, plane - NVX * c, c):
        pair = jnp.floor(0.5 * p)
        m.append((2.0 * pair + 1.0) * (2.0 * (p - 2.0 * pair) - 1.0))
    x, y, z = m
    sq = x * x + y * y + z * z
    quads = [x * x, y * y, z * z, x * y, x * z, y * z]
    cubes = [x * sq, y * sq, z * sq]
    q_hi = [16.0 * jnp.floor((v + 8.0) * 0.0625) for v in quads]
    c_hi = [256.0 * jnp.floor((v + 128.0) * 0.00390625) for v in cubes]
    q_lo = [a - b for a, b in zip(quads, q_hi)]
    c_lo = [a - b for a, b in zip(cubes, c_hi)]
    one, zero = jnp.ones_like(x), jnp.zeros_like(x)
    rows = [one, x, y, z] + q_hi + c_hi + [zero] * 3 + [zero] * 4 + q_lo + c_lo + [zero] * 3
    phi = jnp.concatenate([jnp.where(valid, r, 0.0) for r in rows], axis=0).astype(BF16)
    speeds = [x, y, DT * HALF * x, DT * HALF * jnp.abs(y)]
    return phi, jnp.concatenate(speeds + [zero] * 4, axis=0)


def coefficients(s):
    n, kind, kn = s[0], s[13], s[14]
    rho = WEIGHT * n
    u = [HALF * s[i + 1] / n for i in range(3)]
    h2 = HALF * HALF
    mom = [h2 * s[4 + i] for i in range(6)]
    xx, yy, zz, xy, xz, yz = mom
    energy = xx + yy + zz
    usq = u[0] * u[0] + u[1] * u[1] + u[2] * u[2]
    temp = (energy / n - usq) / 3.0
    second = [[xx, xy, xz], [xy, yy, yz], [xz, yz, zz]]
    q = []
    for i in range(3):
        third = h2 * HALF * s[10 + i]
        mixed = u[0] * second[i][0] + u[1] * second[i][1] + u[2] * second[i][2]
        q.append(0.5 * WEIGHT * (third - 2.0 * mixed - u[i] * energy + 2.0 * n * u[i] * usq))
    keep = jnp.exp(-DT * rho * jnp.sqrt(temp) / kn)
    inv = 1.0 / temp
    tau = 2.0 * math.pi * temp
    front = rho / (tau * jnp.sqrt(tau)) * (1.0 - keep)
    kappa = (1.0 / 3.0) / (5.0 * rho * temp * temp)
    b = usq * inv - 5.0
    uq = u[0] * q[0] + u[1] * q[1] + u[2] * q[2]
    fk = front * kappa
    wall, inflow = kind == 1.0, kind == 2.0
    gas = jnp.logical_not(jnp.logical_or(wall, inflow))
    zero = jnp.zeros_like(n)

    def pick(g, w, i):
        return jnp.where(wall, w, jnp.where(inflow, i, g))

    norm = (2.0 * math.pi) ** -1.5
    arg_sq = pick(-0.5 * h2 * inv, zero - 0.5 * h2, zero - 0.5 * h2)
    arg = [
        pick(-0.5 * usq * inv, zero, zero - 0.125),
        pick(HALF * u[0] * inv, zero, zero + 0.5 * HALF),
        pick(HALF * u[1] * inv, zero, zero),
        pick(HALF * u[2] * inv, zero, zero),
    ] + [arg_sq] * 3 + [zero] * 9
    poly = [pick(front - fk * uq * b, rho * norm, zero + 12.0 * norm)]
    rest = [fk * HALF * (b * q[i] + 2.0 * uq * u[i] * inv) for i in range(3)]
    rest += [-fk * h2 * inv * (2.0 * q[i] * u[i] + uq) for i in range(3)]
    rest += [
        -2.0 * fk * h2 * inv * (q[i] * u[j] + q[j] * u[i]) for i, j in ((0, 1), (0, 2), (1, 2))
    ]
    rest += [fk * h2 * HALF * inv * q[i] for i in range(3)]
    poly += [jnp.where(gas, r, 0.0) for r in rest] + [zero] * 3
    return arg, poly, jnp.where(gas, keep, 0.0)


def pieces(rows):
    whole = jnp.concatenate(rows, axis=0)
    both = jnp.concatenate([whole, whole], axis=0)
    first = both.astype(BF16).astype(F32)
    left = both - first
    second = left.astype(BF16).astype(F32)
    third = left - second
    full = jnp.concatenate([first, second, third, jnp.zeros_like(first)], axis=0)
    return full.T.astype(BF16)


def minmod_pair(mid, a, b):
    lo, hi = jnp.minimum(mid, 0.0), jnp.maximum(mid, 0.0)
    return jnp.minimum(jnp.maximum(a, lo), hi) - jnp.minimum(jnp.maximum(b, lo), hi)


def upwind(pos, far_lo, lo, mid, hi, far_hi):
    before = jnp.where(pos, lo, hi)
    after = jnp.where(pos, hi, lo)
    far = jnp.where(pos, far_lo, far_hi)
    step = mid - before
    return step + 0.5 * minmod_pair(step, after - mid, before - far)


def kernel(
    sizes, count, dist, kind_in, kn_in, out,
    kind_ref, kn_ref, f, g, c_send, y_send, xh, yh, acc, phi_ref, lane_ref,
    arg_c, poly_c, keep_c, arg_h, poly_h, keep_h, ps, sums, y_sums, near,
    cell_sem, in_sem, out_sem, send_sem, recv_sem, ps_send, ps_recv, near_send, near_recv,
):
    nsx, nsy, nvel = sizes
    ncol, nx, ny = f.shape[:3]
    cells = nx * ny
    halo = 4 * (nx + ny)
    halo_pad = arg_h.shape[0]
    first = 2 * ((2 * ncol + 4) // 9)
    more = first + 2 * ncol // 9
    window = more - ncol // 3
    late = ncol - first // 2
    ix, iy, iv = lax.axis_index("sx"), lax.axis_index("sy"), lax.axis_index("vel")
    x_up, x_down = lax.rem(ix + 1, nsx), lax.rem(ix + nsx - 1, nsx)
    y_up, y_down = lax.rem(iy + 1, nsy), lax.rem(iy + nsy - 1, nsy)

    def lanes_of(ref, j):
        return ref.at[:, :, pl.ds(pl.multiple_of(j * LANES, LANES), LANES)]

    def in_copy(j):
        return pltpu.make_async_copy(lanes_of(dist, j), f.at[j], in_sem.at[j])

    def out_copy(j):
        return pltpu.make_async_copy(f.at[j], lanes_of(out, j), out_sem.at[j])

    cell_copies = [
        pltpu.make_async_copy(kind_in, kind_ref, cell_sem.at[0]),
        pltpu.make_async_copy(kn_in, kn_ref, cell_sem.at[1]),
    ]

    @pl.loop(0, ncol)
    def _(j):
        in_copy(j).start()

    for copy in cell_copies:
        copy.start()

    partners = [{"vel": lax.rem(iv + o, nvel)} for o in range(1, nvel)]
    partners += [{"sx": x_up}] + ([{"sx": x_down}] if nsx > 2 else [])
    partners += [{"sy": y_up}] + ([{"sy": y_down}] if nsy > 2 else [])
    barrier = pltpu.get_barrier_semaphore()
    for who in partners:
        pl.semaphore_signal(barrier, inc=1, device_id=who, device_id_type=MESH)

    acc[...] = jnp.zeros_like(acc)
    pl.semaphore_wait(barrier, len(partners))

    def face(slab):
        return pl.ds(slab * PITCH + TOP, ny)

    def halo_copies(step, cols):

        def remote(n, src, dst, who):
            return pltpu.make_async_remote_copy(
                src_ref=src, dst_ref=dst,
                send_sem=send_sem.at[step, cols, n], recv_sem=recv_sem.at[step, cols, n],
                device_id=who, device_id_type=MESH,
            )

        copies = [
            remote(0, f.at[cols, nx - 1], xh.at[step, cols, 1], {"sx": x_up}),
            remote(1, f.at[cols, 0], xh.at[step, cols, 2], {"sx": x_down}),
            remote(2, c_send.at[cols], xh.at[step, cols, 0], {"sx": x_up}),
            remote(3, y_send.at[cols, 1], yh.at[step, cols, 0], {"sy": y_up}),
            remote(4, y_send.at[cols, 0], yh.at[step, cols, 1], {"sy": y_down}),
        ]
        if nsx > 2:
            copies.append(remote(5, c_send.at[cols], xh.at[step, cols, 3], {"sx": x_down}))
        return copies

    def near_copies(step):
        edge = 4 * ny

        def remote(n, src, first, rows, who):
            return pltpu.make_async_remote_copy(
                src_ref=src, dst_ref=near.at[step, pl.ds(first, rows)],
                send_sem=near_send.at[step, n], recv_sem=near_recv.at[step, n],
                device_id=who, device_id_type=MESH,
            )

        return [
            remote(0, sums.at[step, pl.ds(cells - 2 * ny, 2 * ny)], 0, 2 * ny, {"sx": x_up}),
            remote(1, sums.at[step, pl.ds(0, 2 * ny)], 2 * ny, 2 * ny, {"sx": x_down}),
            remote(2, y_sums.at[step, 1], edge, 2 * nx, {"sy": y_up}),
            remote(3, y_sums.at[step, 0], edge + 2 * nx, 2 * nx, {"sy": y_down}),
        ]

    def build_tables(j):
        offset = j * LANES + lax.broadcasted_iota(jnp.int32, (1, LANES), 1)
        phi, lane_ref[j] = tables((iv * count + offset).astype(F32), offset < count)
        phi_ref[j] = jnp.concatenate([phi] * 4, axis=0)

    def pack(j):
        pos = jnp.broadcast_to(lane_ref[j, 0:1, :], (ny, LANES)) > 0.0
        c_send[j] = jnp.where(pos, f[j, nx - 2], f[j, 1])
        for side, row in ((0, 0), (1, ny - 2)):
            for layer in range(2):
                y_send[j, side, layer * nx : (layer + 1) * nx, :] = f[j, :, row + layer, :]

    def add_moments(j):
        wide = phi_ref[j]
        both = jnp.concatenate([wide, wide], axis=1)
        for r in range(0, cells, 128):
            val = f[j, r // ny : (r + 128) // ny].reshape(128, LANES)
            hi = val.astype(BF16)
            lo = (val - hi.astype(F32)).astype(BF16)
            acc[r : r + 128, :] += lax.dot_general(
                jnp.concatenate([hi, lo], axis=1), both,
                (((1,), (1,)), ((), ())), preferred_element_type=F32,
            )

    def exchange(step):
        local = acc[...].T
        ps[step, iv] = local[0:16] + local[16:32]
        copies = []
        for o in range(1, nvel):
            copy = pltpu.make_async_remote_copy(
                src_ref=ps.at[step, iv], dst_ref=ps.at[step, iv],
                send_sem=ps_send.at[step, o], recv_sem=ps_recv.at[step, o],
                device_id={"vel": lax.rem(iv + o, nvel)}, device_id_type=MESH,
            )
            copy.start()
            copies.append(copy)
        for copy in copies:
            copy.wait()
        total = ps[step, 0]
        for v in range(1, nvel):
            total = total + ps[step, v]
        blank = jnp.zeros((113, cells), F32)
        total = jnp.concatenate([total[0:13], kind_row, kn_row, blank], axis=0)
        sums[step] = total.T
        for side, row in ((0, 0), (1, ny - 2)):
            for layer in range(2):
                y_sums[step, side, layer * nx : (layer + 1) * nx, :] = sums[
                    step, pl.ds(row + layer, nx, stride=ny), :
                ]
        for copy in near_copies(step):
            copy.start()
        return total

    def set_coefficients(total, arg_ref, poly_ref, keep_ref):
        arg, poly, keep = coefficients([total[i : i + 1] for i in range(15)])
        arg_ref[...] = pieces(arg)
        poly_ref[...] = pieces(poly)
        keep_ref[...] = jnp.broadcast_to(keep, (LANES, keep.shape[1])).T

    def relax(j):
        wide = phi_ref[j]
        for r in range(0, cells, 128):
            rows = pl.ds(r, 128)
            arg = jnp.dot(arg_c[rows, :], wide, preferred_element_type=F32)
            poly = jnp.dot(poly_c[rows, :], wide, preferred_element_type=F32)
            val = f[j, r // ny : (r + 128) // ny].reshape(128, LANES)
            new = val * keep_c[rows, :] + jnp.exp(arg) * poly
            for i in range(128 // ny):
                g[j, face(r // ny + i + 2), :] = new[i * ny : (i + 1) * ny]

    def relax_halo(step, j):
        wide = phi_ref[j]
        rows = pl.ds(0, halo)
        arg = jnp.dot(arg_h[rows, :], wide, preferred_element_type=F32)
        poly = jnp.dot(poly_h[rows, :], wide, preferred_element_type=F32)
        far_lo = xh[step, j, 0]
        far_hi = far_lo if nsx == 2 else xh[step, j, 3]
        val = jnp.concatenate(
            [far_lo, xh[step, j, 1], xh[step, j, 2], far_hi, yh[step, j, 0], yh[step, j, 1]], axis=0
        )
        new = val * keep_h[rows, :] + jnp.exp(arg) * poly
        for i, slab in enumerate((0, 1, nx + 2, nx + 3)):
            g[j, face(slab), :] = new[i * ny : (i + 1) * ny]
        for i, first in enumerate((-2, -1, ny, ny + 1)):
            at = 4 * ny + i * nx
            g[j, pl.ds(2 * PITCH + TOP + first, nx, stride=PITCH), :] = new[at : at + nx]

    def transport(j):
        half = ny // 2
        lanes = [jnp.broadcast_to(lane_ref[j, i : i + 1, :], (half, LANES)) for i in range(4)]
        pos_x, pos_y = lanes[0] > 0.0, lanes[1] > 0.0
        side_x = jnp.where(pos_x, 0.5, -0.5)
        rate_x, rate_y = lanes[2:]
        for row in (0, half):

            def cells_at(x, d=0):
                return g[j, pl.ds((x + 2) * PITCH + TOP + row + d, half), :]

            low, mid = cells_at(-2), cells_at(-1)
            diff = mid - low
            kept = face_value = flux = None
            for x in range(-1, nx + 1):
                high = cells_at(x + 1)
                ahead = high - mid
                slope = jnp.minimum(
                    jnp.maximum(ahead, jnp.minimum(diff, 0.0)), jnp.maximum(diff, 0.0)
                )
                value = mid + side_x * slope
                if x >= 0:
                    new_flux = jnp.where(pos_x, face_value, value)
                if x >= 1:
                    along = [cells_at(x - 1, d) for d in (-2, -1, 1, 2)]
                    div_y = upwind(pos_y, along[0], along[1], kept, along[2], along[3])
                    f[j, x - 1, row : row + half, :] = kept - (
                        rate_x * (new_flux - flux) + rate_y * div_y
                    )
                if x >= 0:
                    flux = new_flux
                kept, face_value, mid, diff = mid, value, high, ahead

    def send(step, k):
        for copy in halo_copies(step, k):
            copy.start()

    @pl.loop(0, ncol)
    def _(j):
        build_tables(j)
        in_copy(j).wait()
        pack(j)

        @pl.when(j < first)
        def _():
            send(0, j)

        add_moments(j)

    for copy in cell_copies:
        copy.wait()
    kind = kind_ref[...].astype(F32)
    kn = kn_ref[...]
    kind_row = jnp.concatenate([kind[x : x + 1] for x in range(nx)], axis=1)
    kn_row = jnp.concatenate([kn[x : x + 1] for x in range(nx)], axis=1)

    for step in range(STEPS):
        last = step == STEPS - 1
        total = exchange(step)

        @pl.loop(first, more)
        def _(j):
            send(step, j)

        set_coefficients(total, arg_c, poly_c, keep_c)

        @pl.loop(0, ncol)
        def _(j):
            relax(j)

        for copy in near_copies(step):
            copy.wait()
        around = [near[step, 0:halo, :]]
        if halo_pad > halo:
            around.append(sums[step, 0 : halo_pad - halo, :])
        set_coefficients(jnp.concatenate(around, axis=0).T, arg_h, poly_h, keep_h)
        if not last:
            acc[...] = jnp.zeros_like(acc)

        @pl.loop(0, ncol)
        def _(j):
            for copy in halo_copies(step, j):
                copy.wait()

            @pl.when((j >= more - window) & (j < ncol - window))
            def _():
                send(step, j + window)

            relax_halo(step, j)
            transport(j)
            if last:
                out_copy(j).start()
            else:
                pack(j)

                @pl.when(j >= late)
                def _():
                    send(step + 1, 2 * (j - late))
                    send(step + 1, 2 * (j - late) + 1)

                add_moments(j)

    @pl.loop(0, ncol)
    def _(j):
        out_copy(j).wait()


def body(sizes, distribution, cell_kind, local_knudsen):
    nx, ny, count = distribution.shape
    ncol = -(-count // LANES)
    width = ncol * LANES
    padded = distribution
    if width != count:
        padded = jnp.pad(distribution, ((0, 0), (0, 0), (0, width - count)))
    cells = nx * ny
    halo_pad = -(-4 * (nx + ny) // LANES) * LANES
    nsx, nsy, nvel = sizes
    xcopies = 3 if nsx == 2 else 4
    dma = pltpu.SemaphoreType.DMA
    operands = [
        pltpu.with_memory_space_constraint(a, pltpu.MemorySpace.HBM)
        for a in (padded, cell_kind, local_knudsen)
    ]
    result = pl.pallas_call(
        functools.partial(kernel, sizes, count),
        out_shape=jax.ShapeDtypeStruct((nx, ny, width), F32),
        in_specs=[pl.BlockSpec(memory_space=pltpu.MemorySpace.HBM)] * 3,
        out_specs=pl.BlockSpec(memory_space=pl.ANY),
        scratch_shapes=[
            pltpu.VMEM((nx, ny), jnp.int32),
            pltpu.VMEM((nx, ny), F32),
            pltpu.VMEM((ncol, nx, ny, LANES), F32),
            pltpu.VMEM((ncol, (nx + 4) * PITCH, LANES), F32),
            pltpu.VMEM((ncol, ny, LANES), F32),
            pltpu.VMEM((ncol, 2, 2 * nx, LANES), F32),
            pltpu.VMEM((STEPS, ncol, xcopies, ny, LANES), F32),
            pltpu.VMEM((STEPS, ncol, 2, 2 * nx, LANES), F32),
            pltpu.VMEM((cells, LANES), F32),
            pltpu.VMEM((ncol, LANES, LANES), BF16),
            pltpu.VMEM((ncol, 8, LANES), F32),
            pltpu.VMEM((cells, LANES), BF16),
            pltpu.VMEM((cells, LANES), BF16),
            pltpu.VMEM((cells, LANES), F32),
            pltpu.VMEM((halo_pad, LANES), BF16),
            pltpu.VMEM((halo_pad, LANES), BF16),
            pltpu.VMEM((halo_pad, LANES), F32),
            pltpu.VMEM((STEPS, nvel, 16, cells), F32),
            pltpu.VMEM((STEPS, cells, LANES), F32),
            pltpu.VMEM((STEPS, 2, 2 * nx, LANES), F32),
            pltpu.VMEM((STEPS, 4 * (nx + ny), LANES), F32),
            dma((2,)),
            dma((ncol,)),
            dma((ncol,)),
            dma((STEPS, ncol, xcopies + 2)),
            dma((STEPS, ncol, xcopies + 2)),
            dma((STEPS, nvel)),
            dma((STEPS, nvel)),
            dma((STEPS, 4)),
            dma((STEPS, 4)),
        ],
        compiler_params=pltpu.CompilerParams(
            collective_id=0, has_side_effects=True, vmem_limit_bytes=40 * 2**20
        ),
    )(*operands)
    return result[..., :count] if width != count else result


def solution(mesh):
    sizes = (mesh.shape["sx"], mesh.shape["sy"], mesh.shape["vel"])
    return jax.shard_map(
        functools.partial(body, sizes),
        mesh=mesh,
        in_specs=(P("sx", "sy", "vel"), P("sx", "sy"), P("sx", "sy")),
        out_specs=P("sx", "sy", "vel"),
        check_vma=False,
    )
```

```python
import functools
import math

import jax
import jax.numpy as jnp
from jax import lax
from jax.experimental import pallas as pl
from jax.experimental.pallas import tpu as pltpu
from jax.sharding import PartitionSpec as P

NVX = 24
STEPS = 2
VEL_LIMIT = 4.8
DT = 0.09
SPACING = 2.0 * VEL_LIMIT / NVX
HALF = 0.5 * SPACING
WEIGHT = SPACING**3
LANES = 128
PITCH = 48
TOP = 8
MESH = pl.DeviceIdType.MESH
F32 = jnp.float32
BF16 = jnp.bfloat16


def tables(index, valid):
    plane = jnp.floor((index + 0.5) * (1.0 / NVX))
    c = jnp.floor((plane + 0.5) * (1.0 / NVX))
    m = []
    for p in (index - NVX * plane, plane - NVX * c, c):
        pair = jnp.floor(0.5 * p)
        m.append((2.0 * pair + 1.0) * (2.0 * (p - 2.0 * pair) - 1.0))
    x, y, z = m
    sq = x * x + y * y + z * z
    quads = [x * x, y * y, z * z, x * y, x * z, y * z]
    cubes = [x * sq, y * sq, z * sq]
    q_hi = [16.0 * jnp.floor((v + 8.0) * 0.0625) for v in quads]
    c_hi = [256.0 * jnp.floor((v + 128.0) * 0.00390625) for v in cubes]
    q_lo = [a - b for a, b in zip(quads, q_hi)]
    c_lo = [a - b for a, b in zip(cubes, c_hi)]
    one, zero = jnp.ones_like(x), jnp.zeros_like(x)
    rows = [one, x, y, z] + q_hi + c_hi + [zero] * 3 + [zero] * 4 + q_lo + c_lo + [zero] * 3
    phi = jnp.concatenate([jnp.where(valid, r, 0.0) for r in rows], axis=0).astype(BF16)
    speeds = [x, y, DT * HALF * x, DT * HALF * jnp.abs(y)]
    return phi, jnp.concatenate(speeds + [zero] * 4, axis=0)


def coefficients(s):
    n, kind, kn = s[0], s[13], s[14]
    rho = WEIGHT * n
    u = [HALF * s[i + 1] / n for i in range(3)]
    h2 = HALF * HALF
    mom = [h2 * s[4 + i] for i in range(6)]
    xx, yy, zz, xy, xz, yz = mom
    energy = xx + yy + zz
    usq = u[0] * u[0] + u[1] * u[1] + u[2] * u[2]
    temp = (energy / n - usq) / 3.0
    second = [[xx, xy, xz], [xy, yy, yz], [xz, yz, zz]]
    q = []
    for i in range(3):
        third = h2 * HALF * s[10 + i]
        mixed = u[0] * second[i][0] + u[1] * second[i][1] + u[2] * second[i][2]
        q.append(0.5 * WEIGHT * (third - 2.0 * mixed - u[i] * energy + 2.0 * n * u[i] * usq))
    keep = jnp.exp(-DT * rho * jnp.sqrt(temp) / kn)
    inv = 1.0 / temp
    tau = 2.0 * math.pi * temp
    front = rho / (tau * jnp.sqrt(tau)) * (1.0 - keep)
    kappa = (1.0 / 3.0) / (5.0 * rho * temp * temp)
    b = usq * inv - 5.0
    uq = u[0] * q[0] + u[1] * q[1] + u[2] * q[2]
    fk = front * kappa
    wall, inflow = kind == 1.0, kind == 2.0
    gas = jnp.logical_not(jnp.logical_or(wall, inflow))
    zero = jnp.zeros_like(n)

    def pick(g, w, i):
        return jnp.where(wall, w, jnp.where(inflow, i, g))

    norm = (2.0 * math.pi) ** -1.5
    arg_sq = pick(-0.5 * h2 * inv, zero - 0.5 * h2, zero - 0.5 * h2)
    arg = [
        pick(-0.5 * usq * inv, zero, zero - 0.125),
        pick(HALF * u[0] * inv, zero, zero + 0.5 * HALF),
        pick(HALF * u[1] * inv, zero, zero),
        pick(HALF * u[2] * inv, zero, zero),
    ] + [arg_sq] * 3 + [zero] * 9
    poly = [pick(front - fk * uq * b, rho * norm, zero + 12.0 * norm)]
    rest = [fk * HALF * (b * q[i] + 2.0 * uq * u[i] * inv) for i in range(3)]
    rest += [-fk * h2 * inv * (2.0 * q[i] * u[i] + uq) for i in range(3)]
    rest += [
        -2.0 * fk * h2 * inv * (q[i] * u[j] + q[j] * u[i]) for i, j in ((0, 1), (0, 2), (1, 2))
    ]
    rest += [fk * h2 * HALF * inv * q[i] for i in range(3)]
    poly += [jnp.where(gas, r, 0.0) for r in rest] + [zero] * 3
    return arg, poly, jnp.where(gas, keep, 0.0)


def pieces(rows):
    whole = jnp.concatenate(rows, axis=0)
    both = jnp.concatenate([whole, whole], axis=0)
    first = both.astype(BF16).astype(F32)
    left = both - first
    second = left.astype(BF16).astype(F32)
    third = left - second
    full = jnp.concatenate([first, second, third, jnp.zeros_like(first)], axis=0)
    return full.T.astype(BF16)


def minmod_pair(mid, a, b):
    lo, hi = jnp.minimum(mid, 0.0), jnp.maximum(mid, 0.0)
    return jnp.minimum(jnp.maximum(a, lo), hi) - jnp.minimum(jnp.maximum(b, lo), hi)


def upwind(pos, far_lo, lo, mid, hi, far_hi):
    before = jnp.where(pos, lo, hi)
    after = jnp.where(pos, hi, lo)
    far = jnp.where(pos, far_lo, far_hi)
    step = mid - before
    return step + 0.5 * minmod_pair(step, after - mid, before - far)


def kernel(
    sizes, group, head, count, dist, kind_in, kn_in, out,
    kind_ref, kn_ref, f, g, x_send, y_send, xh, yh, acc, phi_ref, lane_ref,
    arg_c, poly_c, keep_c, arg_h, poly_h, keep_h, ps, sums, y_sums, near,
    cell_sem, in_sem, out_sem, send_sem, recv_sem, ps_send, ps_recv, near_send, near_recv,
):
    nsx, nsy, nvel = sizes
    ncol, nx, ny = f.shape[:3]
    cells = nx * ny
    halo = 4 * (nx + ny)
    halo_pad = arg_h.shape[0]
    groups = ncol // group
    ix, iy, iv = lax.axis_index("sx"), lax.axis_index("sy"), lax.axis_index("vel")
    x_up, x_down = lax.rem(ix + 1, nsx), lax.rem(ix + nsx - 1, nsx)
    y_up, y_down = lax.rem(iy + 1, nsy), lax.rem(iy + nsy - 1, nsy)

    def lanes_of(ref, j):
        return ref.at[:, :, pl.ds(pl.multiple_of(j * LANES, LANES), LANES)]

    def in_copy(j):
        return pltpu.make_async_copy(lanes_of(dist, j), f.at[j], in_sem.at[j])

    def out_copy(j):
        return pltpu.make_async_copy(f.at[j], lanes_of(out, j), out_sem.at[j])

    cell_copies = [
        pltpu.make_async_copy(kind_in, kind_ref, cell_sem.at[0]),
        pltpu.make_async_copy(kn_in, kn_ref, cell_sem.at[1]),
    ]

    @pl.loop(0, ncol)
    def _(j):
        in_copy(j).start()

    for copy in cell_copies:
        copy.start()

    partners = [{"vel": lax.rem(iv + o, nvel)} for o in range(1, nvel)]
    partners += [{"sx": x_up}] + ([{"sx": x_down}] if nsx > 2 else [])
    partners += [{"sy": y_up}] + ([{"sy": y_down}] if nsy > 2 else [])
    barrier = pltpu.get_barrier_semaphore()
    for who in partners:
        pl.semaphore_signal(barrier, inc=1, device_id=who, device_id_type=MESH)

    acc[...] = jnp.zeros_like(acc)

    def face(slab):
        return pl.ds(slab * PITCH + TOP, ny)

    def halo_copies(step, k):
        cols = pl.ds(k * group, group)

        def remote(n, src, dst, who):
            return pltpu.make_async_remote_copy(
                src_ref=src, dst_ref=dst,
                send_sem=send_sem.at[step, k, n], recv_sem=recv_sem.at[step, k, n],
                device_id=who, device_id_type=MESH,
            )

        copies = [
            remote(0, y_send.at[cols, 1], yh.at[step, cols, 0], {"sy": y_up}),
            remote(1, y_send.at[cols, 0], yh.at[step, cols, 1], {"sy": y_down}),
        ]
        if nsx == 2:
            return [remote(2, x_send.at[cols], xh.at[step, cols], {"sx": x_up})] + copies
        copies += [
            remote(2, x_send.at[cols, 0], xh.at[step, cols, 0], {"sx": x_up}),
            remote(3, x_send.at[cols, 1], xh.at[step, cols, 1], {"sx": x_up}),
            remote(4, x_send.at[cols, 2], xh.at[step, cols, 2], {"sx": x_down}),
            remote(5, x_send.at[cols, 0], xh.at[step, cols, 3], {"sx": x_down}),
        ]
        return copies

    def near_copies(step):
        edge = 4 * ny

        def remote(n, src, first, rows, who):
            return pltpu.make_async_remote_copy(
                src_ref=src, dst_ref=near.at[step, pl.ds(first, rows)],
                send_sem=near_send.at[step, n], recv_sem=near_recv.at[step, n],
                device_id=who, device_id_type=MESH,
            )

        return [
            remote(0, sums.at[step, pl.ds(cells - 2 * ny, 2 * ny)], 0, 2 * ny, {"sx": x_up}),
            remote(1, sums.at[step, pl.ds(0, 2 * ny)], 2 * ny, 2 * ny, {"sx": x_down}),
            remote(2, y_sums.at[step, 1], edge, 2 * nx, {"sy": y_up}),
            remote(3, y_sums.at[step, 0], edge + 2 * nx, 2 * nx, {"sy": y_down}),
        ]

    def build_tables(j):
        offset = j * LANES + lax.broadcasted_iota(jnp.int32, (1, LANES), 1)
        phi, lane_ref[j] = tables((iv * count + offset).astype(F32), offset < count)
        phi_ref[j] = jnp.concatenate([phi] * 4, axis=0)

    def pack(j):
        pos = jnp.broadcast_to(lane_ref[j, 0:1, :], (ny, LANES)) > 0.0
        x_send[j, 0] = jnp.where(pos, f[j, nx - 2], f[j, 1])
        x_send[j, 1] = f[j, nx - 1]
        x_send[j, 2] = f[j, 0]
        for side, first in ((0, 0), (1, ny - 2)):
            for layer in range(2):
                y_send[j, side, layer * nx : (layer + 1) * nx, :] = f[j, :, first + layer, :]

    def add_moments(j):
        wide = phi_ref[j]
        both = jnp.concatenate([wide, wide], axis=1)
        for r in range(0, cells, 128):
            val = f[j, r // ny : (r + 128) // ny].reshape(128, LANES)
            hi = val.astype(BF16)
            lo = (val - hi.astype(F32)).astype(BF16)
            acc[r : r + 128, :] += lax.dot_general(
                jnp.concatenate([hi, lo], axis=1), both,
                (((1,), (1,)), ((), ())), preferred_element_type=F32,
            )

    def exchange(step):
        local = acc[...].T
        ps[step, iv] = local[0:16] + local[16:32]
        copies = []
        for o in range(1, nvel):
            copy = pltpu.make_async_remote_copy(
                src_ref=ps.at[step, iv], dst_ref=ps.at[step, iv],
                send_sem=ps_send.at[step, o], recv_sem=ps_recv.at[step, o],
                device_id={"vel": lax.rem(iv + o, nvel)}, device_id_type=MESH,
            )
            copy.start()
            copies.append(copy)
        for copy in copies:
            copy.wait()
        total = ps[step, 0]
        for v in range(1, nvel):
            total = total + ps[step, v]
        blank = jnp.zeros((113, cells), F32)
        total = jnp.concatenate([total[0:13], kind_row, kn_row, blank], axis=0)
        sums[step] = total.T
        for side, first in ((0, 0), (1, ny - 2)):
            for layer in range(2):
                y_sums[step, side, layer * nx : (layer + 1) * nx, :] = sums[
                    step, pl.ds(first + layer, nx, stride=ny), :
                ]
        for copy in near_copies(step):
            copy.start()
        return total

    def set_coefficients(total, arg_ref, poly_ref, keep_ref):
        arg, poly, keep = coefficients([total[i : i + 1] for i in range(15)])
        arg_ref[...] = pieces(arg)
        poly_ref[...] = pieces(poly)
        keep_ref[...] = jnp.broadcast_to(keep, (LANES, keep.shape[1])).T

    def relax(j):
        wide = phi_ref[j]
        for r in range(0, cells, 128):
            rows = pl.ds(r, 128)
            arg = jnp.dot(arg_c[rows, :], wide, preferred_element_type=F32)
            poly = jnp.dot(poly_c[rows, :], wide, preferred_element_type=F32)
            val = f[j, r // ny : (r + 128) // ny].reshape(128, LANES)
            new = val * keep_c[rows, :] + jnp.exp(arg) * poly
            for i in range(128 // ny):
                g[j, face(r // ny + i + 2), :] = new[i * ny : (i + 1) * ny]

    def relax_halo(step, j):
        wide = phi_ref[j]
        rows = pl.ds(0, halo)
        arg = jnp.dot(arg_h[rows, :], wide, preferred_element_type=F32)
        poly = jnp.dot(poly_h[rows, :], wide, preferred_element_type=F32)
        far_lo = xh[step, j, 0]
        far_hi = far_lo if nsx == 2 else xh[step, j, 3]
        val = jnp.concatenate(
            [far_lo, xh[step, j, 1], xh[step, j, 2], far_hi, yh[step, j, 0], yh[step, j, 1]], axis=0
        )
        new = val * keep_h[rows, :] + jnp.exp(arg) * poly
        for i, slab in enumerate((0, 1, nx + 2, nx + 3)):
            g[j, face(slab), :] = new[i * ny : (i + 1) * ny]
        for i, first in enumerate((-2, -1, ny, ny + 1)):
            at = 4 * ny + i * nx
            g[j, pl.ds(2 * PITCH + TOP + first, nx, stride=PITCH), :] = new[at : at + nx]

    def transport(j):
        half = ny // 2
        lanes = [jnp.broadcast_to(lane_ref[j, i : i + 1, :], (half, LANES)) for i in range(4)]
        pos_x, pos_y = lanes[0] > 0.0, lanes[1] > 0.0
        side_x = jnp.where(pos_x, 0.5, -0.5)
        rate_x, rate_y = lanes[2:]
        for row in (0, half):

            def cells_at(x, d=0):
                return g[j, pl.ds((x + 2) * PITCH + TOP + row + d, half), :]

            low, mid = cells_at(-2), cells_at(-1)
            diff = mid - low
            kept = face_value = flux = None
            for x in range(-1, nx + 1):
                high = cells_at(x + 1)
                ahead = high - mid
                slope = jnp.minimum(
                    jnp.maximum(ahead, jnp.minimum(diff, 0.0)), jnp.maximum(diff, 0.0)
                )
                value = mid + side_x * slope
                if x >= 0:
                    new_flux = jnp.where(pos_x, face_value, value)
                if x >= 1:
                    along = [cells_at(x - 1, d) for d in (-2, -1, 1, 2)]
                    div_y = upwind(pos_y, along[0], along[1], kept, along[2], along[3])
                    f[j, x - 1, row : row + half, :] = kept - (
                        rate_x * (new_flux - flux) + rate_y * div_y
                    )
                if x >= 0:
                    flux = new_flux
                kept, face_value, mid, diff = mid, value, high, ahead

    def send(step, k):
        for copy in halo_copies(step, k):
            copy.start()

    def prepare(k):
        @pl.loop(0, group)
        def _(i):
            j = k * group + i
            build_tables(j)
            in_copy(j).wait()
            pack(j)

    prepare(0)
    pl.semaphore_wait(barrier, len(partners))

    @pl.loop(0, groups)
    def _(k):
        @pl.when(k > 0)
        def _():
            prepare(k)

        @pl.when(k < head)
        def _():
            send(0, k)

        @pl.loop(0, group)
        def _(i):
            add_moments(k * group + i)

    for copy in cell_copies:
        copy.wait()
    kind = kind_ref[...].astype(F32)
    kn = kn_ref[...]
    kind_row = jnp.concatenate([kind[x : x + 1] for x in range(nx)], axis=1)
    kn_row = jnp.concatenate([kn[x : x + 1] for x in range(nx)], axis=1)

    for step in range(STEPS):
        last = step == STEPS - 1
        total = exchange(step)

        @pl.loop(head, groups)
        def _(k):
            send(step, k)

        set_coefficients(total, arg_c, poly_c, keep_c)

        @pl.loop(0, ncol)
        def _(j):
            relax(j)

        for copy in near_copies(step):
            copy.wait()
        around = [near[step, 0:halo, :]]
        if halo_pad > halo:
            around.append(sums[step, 0 : halo_pad - halo, :])
        set_coefficients(jnp.concatenate(around, axis=0).T, arg_h, poly_h, keep_h)
        if not last:
            acc[...] = jnp.zeros_like(acc)

        @pl.loop(0, groups)
        def _(k):
            for copy in halo_copies(step, k):
                copy.wait()

            @pl.loop(0, group)
            def _(i):
                j = k * group + i
                relax_halo(step, j)
                transport(j)
                if last:
                    out_copy(j).start()
                else:
                    pack(j)

            if not last:
                @pl.when(k < head)
                def _():
                    send(step + 1, k)

                @pl.loop(0, group)
                def _(i):
                    add_moments(k * group + i)

    @pl.loop(0, ncol)
    def _(j):
        out_copy(j).wait()


def body(sizes, distribution, cell_kind, local_knudsen):
    nx, ny, count = distribution.shape
    ncol = -(-count // LANES)
    width = ncol * LANES
    padded = distribution
    if width != count:
        padded = jnp.pad(distribution, ((0, 0), (0, 0), (0, width - count)))
    group = 3 if ncol % 3 == 0 else 1
    groups, cells = ncol // group, nx * ny
    halo_pad = -(-4 * (nx + ny) // LANES) * LANES
    head = (4 * groups + 8) // 9
    nsx, nsy, nvel = sizes
    xcopies = 3 if nsx == 2 else 4
    dma = pltpu.SemaphoreType.DMA
    operands = [
        pltpu.with_memory_space_constraint(a, pltpu.MemorySpace.HBM)
        for a in (padded, cell_kind, local_knudsen)
    ]
    result = pl.pallas_call(
        functools.partial(kernel, sizes, group, head, count),
        out_shape=jax.ShapeDtypeStruct((nx, ny, width), F32),
        in_specs=[pl.BlockSpec(memory_space=pltpu.MemorySpace.HBM)] * 3,
        out_specs=pl.BlockSpec(memory_space=pl.ANY),
        scratch_shapes=[
            pltpu.VMEM((nx, ny), jnp.int32),
            pltpu.VMEM((nx, ny), F32),
            pltpu.VMEM((ncol, nx, ny, LANES), F32),
            pltpu.VMEM((ncol, (nx + 4) * PITCH, LANES), F32),
            pltpu.VMEM((ncol, 3, ny, LANES), F32),
            pltpu.VMEM((ncol, 2, 2 * nx, LANES), F32),
            pltpu.VMEM((STEPS, ncol, xcopies, ny, LANES), F32),
            pltpu.VMEM((STEPS, ncol, 2, 2 * nx, LANES), F32),
            pltpu.VMEM((cells, LANES), F32),
            pltpu.VMEM((ncol, LANES, LANES), BF16),
            pltpu.VMEM((ncol, 8, LANES), F32),
            pltpu.VMEM((cells, LANES), BF16),
            pltpu.VMEM((cells, LANES), BF16),
            pltpu.VMEM((cells, LANES), F32),
            pltpu.VMEM((halo_pad, LANES), BF16),
            pltpu.VMEM((halo_pad, LANES), BF16),
            pltpu.VMEM((halo_pad, LANES), F32),
            pltpu.VMEM((STEPS, nvel, 16, cells), F32),
            pltpu.VMEM((STEPS, cells, LANES), F32),
            pltpu.VMEM((STEPS, 2, 2 * nx, LANES), F32),
            pltpu.VMEM((STEPS, 4 * (nx + ny), LANES), F32),
            dma((2,)),
            dma((ncol,)),
            dma((ncol,)),
            dma((STEPS, groups, 3 if nsx == 2 else 6)),
            dma((STEPS, groups, 3 if nsx == 2 else 6)),
            dma((STEPS, nvel)),
            dma((STEPS, nvel)),
            dma((STEPS, 4)),
            dma((STEPS, 4)),
        ],
        compiler_params=pltpu.CompilerParams(
            collective_id=0, has_side_effects=True, vmem_limit_bytes=40 * 2**20
        ),
    )(*operands)
    return result[..., :count] if width != count else result


def solution(mesh):
    sizes = (mesh.shape["sx"], mesh.shape["sy"], mesh.shape["vel"])
    return jax.shard_map(
        functools.partial(body, sizes),
        mesh=mesh,
        in_specs=(P("sx", "sy", "vel"), P("sx", "sy"), P("sx", "sy")),
        out_specs=P("sx", "sy", "vel"),
        check_vma=False,
    )
```

```python
import functools
import math

import jax
import jax.numpy as jnp
from jax import lax
from jax.experimental import pallas as pl
from jax.experimental.pallas import tpu as pltpu
from jax.sharding import PartitionSpec as P

NVX = 24
STEPS = 2
VEL_LIMIT = 4.8
DT = 0.09
SPACING = 2.0 * VEL_LIMIT / NVX
HALF = 0.5 * SPACING
WEIGHT = SPACING**3
LANES = 128
PITCH = 48
TOP = 8
MESH = pl.DeviceIdType.MESH
F32 = jnp.float32
BF16 = jnp.bfloat16


def tables(index, valid):
    plane = jnp.floor((index + 0.5) * (1.0 / NVX))
    c = jnp.floor((plane + 0.5) * (1.0 / NVX))
    m = []
    for p in (index - NVX * plane, plane - NVX * c, c):
        pair = jnp.floor(0.5 * p)
        m.append((2.0 * pair + 1.0) * (2.0 * (p - 2.0 * pair) - 1.0))
    x, y, z = m
    sq = x * x + y * y + z * z
    quads = [x * x, y * y, z * z, x * y, x * z, y * z]
    cubes = [x * sq, y * sq, z * sq]
    q_hi = [16.0 * jnp.floor((v + 8.0) * 0.0625) for v in quads]
    c_hi = [256.0 * jnp.floor((v + 128.0) * 0.00390625) for v in cubes]
    q_lo = [a - b for a, b in zip(quads, q_hi)]
    c_lo = [a - b for a, b in zip(cubes, c_hi)]
    one, zero = jnp.ones_like(x), jnp.zeros_like(x)
    rows = [one, x, y, z] + q_hi + c_hi + [zero] * 3 + [zero] * 4 + q_lo + c_lo + [zero] * 3
    phi = jnp.concatenate([jnp.where(valid, r, 0.0) for r in rows], axis=0).astype(BF16)
    speeds = [x, y, DT * HALF * x, DT * HALF * jnp.abs(y)]
    return phi, jnp.concatenate(speeds + [zero] * 4, axis=0)


def coefficients(s):
    n, kind, kn = s[0], s[13], s[14]
    rho = WEIGHT * n
    u = [HALF * s[i + 1] / n for i in range(3)]
    h2 = HALF * HALF
    mom = [h2 * s[4 + i] for i in range(6)]
    xx, yy, zz, xy, xz, yz = mom
    energy = xx + yy + zz
    usq = u[0] * u[0] + u[1] * u[1] + u[2] * u[2]
    temp = (energy / n - usq) / 3.0
    second = [[xx, xy, xz], [xy, yy, yz], [xz, yz, zz]]
    q = []
    for i in range(3):
        third = h2 * HALF * s[10 + i]
        mixed = u[0] * second[i][0] + u[1] * second[i][1] + u[2] * second[i][2]
        q.append(0.5 * WEIGHT * (third - 2.0 * mixed - u[i] * energy + 2.0 * n * u[i] * usq))
    keep = jnp.exp(-DT * rho * jnp.sqrt(temp) / kn)
    inv = 1.0 / temp
    tau = 2.0 * math.pi * temp
    front = rho / (tau * jnp.sqrt(tau)) * (1.0 - keep)
    kappa = (1.0 / 3.0) / (5.0 * rho * temp * temp)
    b = usq * inv - 5.0
    uq = u[0] * q[0] + u[1] * q[1] + u[2] * q[2]
    fk = front * kappa
    wall, inflow = kind == 1.0, kind == 2.0
    gas = jnp.logical_not(jnp.logical_or(wall, inflow))
    zero = jnp.zeros_like(n)

    def pick(g, w, i):
        return jnp.where(wall, w, jnp.where(inflow, i, g))

    norm = (2.0 * math.pi) ** -1.5
    arg_sq = pick(-0.5 * h2 * inv, zero - 0.5 * h2, zero - 0.5 * h2)
    arg = [
        pick(-0.5 * usq * inv, zero, zero - 0.125),
        pick(HALF * u[0] * inv, zero, zero + 0.5 * HALF),
        pick(HALF * u[1] * inv, zero, zero),
        pick(HALF * u[2] * inv, zero, zero),
    ] + [arg_sq] * 3 + [zero] * 9
    poly = [pick(front - fk * uq * b, rho * norm, zero + 12.0 * norm)]
    rest = [fk * HALF * (b * q[i] + 2.0 * uq * u[i] * inv) for i in range(3)]
    rest += [-fk * h2 * inv * (2.0 * q[i] * u[i] + uq) for i in range(3)]
    rest += [
        -2.0 * fk * h2 * inv * (q[i] * u[j] + q[j] * u[i]) for i, j in ((0, 1), (0, 2), (1, 2))
    ]
    rest += [fk * h2 * HALF * inv * q[i] for i in range(3)]
    poly += [jnp.where(gas, r, 0.0) for r in rest] + [zero] * 3
    return arg, poly, jnp.where(gas, keep, 0.0)


def pieces(rows):
    whole = jnp.concatenate(rows, axis=0)
    both = jnp.concatenate([whole, whole], axis=0)
    first = both.astype(BF16).astype(F32)
    left = both - first
    second = left.astype(BF16).astype(F32)
    third = left - second
    full = jnp.concatenate([first, second, third, jnp.zeros_like(first)], axis=0)
    return full.T.astype(BF16)


def minmod_pair(mid, a, b):
    lo, hi = jnp.minimum(mid, 0.0), jnp.maximum(mid, 0.0)
    return jnp.minimum(jnp.maximum(a, lo), hi) - jnp.minimum(jnp.maximum(b, lo), hi)


def upwind(pos, far_lo, lo, mid, hi, far_hi):
    before = jnp.where(pos, lo, hi)
    after = jnp.where(pos, hi, lo)
    far = jnp.where(pos, far_lo, far_hi)
    step = mid - before
    return step + 0.5 * minmod_pair(step, after - mid, before - far)


def kernel(
    sizes, group, head, count, dist, kind_in, kn_in, out,
    kind_ref, kn_ref, f, g, x_send, y_send, xh, yh, acc, phi_ref, lane_ref,
    arg_c, poly_c, keep_c, arg_h, poly_h, keep_h, ps, sums, y_sums, near,
    cell_sem, in_sem, out_sem, send_sem, recv_sem, ps_send, ps_recv, near_send, near_recv,
):
    nsx, nsy, nvel = sizes
    ncol, nx, ny = f.shape[:3]
    cells = nx * ny
    halo = 4 * (nx + ny)
    halo_pad = arg_h.shape[0]
    groups = ncol // group
    ix, iy, iv = lax.axis_index("sx"), lax.axis_index("sy"), lax.axis_index("vel")
    x_up, x_down = lax.rem(ix + 1, nsx), lax.rem(ix + nsx - 1, nsx)
    y_up, y_down = lax.rem(iy + 1, nsy), lax.rem(iy + nsy - 1, nsy)

    def lanes_of(ref, j):
        return ref.at[:, :, pl.ds(pl.multiple_of(j * LANES, LANES), LANES)]

    def in_copy(j):
        return pltpu.make_async_copy(lanes_of(dist, j), f.at[j], in_sem.at[j])

    def out_copy(j):
        return pltpu.make_async_copy(f.at[j], lanes_of(out, j), out_sem.at[j])

    cell_copies = [
        pltpu.make_async_copy(kind_in, kind_ref, cell_sem.at[0]),
        pltpu.make_async_copy(kn_in, kn_ref, cell_sem.at[1]),
    ]

    @pl.loop(0, ncol)
    def _(j):
        in_copy(j).start()

    for copy in cell_copies:
        copy.start()

    partners = [{"vel": lax.rem(iv + o, nvel)} for o in range(1, nvel)]
    partners += [{"sx": x_up}] + ([{"sx": x_down}] if nsx > 2 else [])
    partners += [{"sy": y_up}] + ([{"sy": y_down}] if nsy > 2 else [])
    barrier = pltpu.get_barrier_semaphore()
    for who in partners:
        pl.semaphore_signal(barrier, inc=1, device_id=who, device_id_type=MESH)

    acc[...] = jnp.zeros_like(acc)

    def face(slab):
        return pl.ds(slab * PITCH + TOP, ny)

    def halo_copies(step, k, tail=None):
        cols = pl.ds(k * group, group) if tail is None else pl.ds(k * group + tail, 1)
        slot = k if tail is None else k + tail

        def remote(n, src, dst, who):
            return pltpu.make_async_remote_copy(
                src_ref=src, dst_ref=dst,
                send_sem=send_sem.at[step, slot, n], recv_sem=recv_sem.at[step, slot, n],
                device_id=who, device_id_type=MESH,
            )

        copies = [
            remote(0, y_send.at[cols, 1], yh.at[step, cols, 0], {"sy": y_up}),
            remote(1, y_send.at[cols, 0], yh.at[step, cols, 1], {"sy": y_down}),
        ]
        if nsx == 2:
            return [remote(2, x_send.at[cols], xh.at[step, cols], {"sx": x_up})] + copies
        copies += [
            remote(2, x_send.at[cols, 0], xh.at[step, cols, 0], {"sx": x_up}),
            remote(3, x_send.at[cols, 1], xh.at[step, cols, 1], {"sx": x_up}),
            remote(4, x_send.at[cols, 2], xh.at[step, cols, 2], {"sx": x_down}),
            remote(5, x_send.at[cols, 0], xh.at[step, cols, 3], {"sx": x_down}),
        ]
        return copies

    def near_copies(step):
        edge = 4 * ny

        def remote(n, src, first, rows, who):
            return pltpu.make_async_remote_copy(
                src_ref=src, dst_ref=near.at[step, pl.ds(first, rows)],
                send_sem=near_send.at[step, n], recv_sem=near_recv.at[step, n],
                device_id=who, device_id_type=MESH,
            )

        return [
            remote(0, sums.at[step, pl.ds(cells - 2 * ny, 2 * ny)], 0, 2 * ny, {"sx": x_up}),
            remote(1, sums.at[step, pl.ds(0, 2 * ny)], 2 * ny, 2 * ny, {"sx": x_down}),
            remote(2, y_sums.at[step, 1], edge, 2 * nx, {"sy": y_up}),
            remote(3, y_sums.at[step, 0], edge + 2 * nx, 2 * nx, {"sy": y_down}),
        ]

    def build_tables(j):
        offset = j * LANES + lax.broadcasted_iota(jnp.int32, (1, LANES), 1)
        phi, lane_ref[j] = tables((iv * count + offset).astype(F32), offset < count)
        phi_ref[j] = jnp.concatenate([phi] * 4, axis=0)

    def pack(j):
        pos = jnp.broadcast_to(lane_ref[j, 0:1, :], (ny, LANES)) > 0.0
        x_send[j, 0] = jnp.where(pos, f[j, nx - 2], f[j, 1])
        x_send[j, 1] = f[j, nx - 1]
        x_send[j, 2] = f[j, 0]
        for side, first in ((0, 0), (1, ny - 2)):
            for layer in range(2):
                y_send[j, side, layer * nx : (layer + 1) * nx, :] = f[j, :, first + layer, :]

    def add_moments(j):
        wide = phi_ref[j]
        both = jnp.concatenate([wide, wide], axis=1)
        for r in range(0, cells, 128):
            val = f[j, r // ny : (r + 128) // ny].reshape(128, LANES)
            hi = val.astype(BF16)
            lo = (val - hi.astype(F32)).astype(BF16)
            acc[r : r + 128, :] += lax.dot_general(
                jnp.concatenate([hi, lo], axis=1), both,
                (((1,), (1,)), ((), ())), preferred_element_type=F32,
            )

    def exchange(step):
        local = acc[...].T
        ps[step, iv] = local[0:16] + local[16:32]
        copies = []
        for o in range(1, nvel):
            copy = pltpu.make_async_remote_copy(
                src_ref=ps.at[step, iv], dst_ref=ps.at[step, iv],
                send_sem=ps_send.at[step, o], recv_sem=ps_recv.at[step, o],
                device_id={"vel": lax.rem(iv + o, nvel)}, device_id_type=MESH,
            )
            copy.start()
            copies.append(copy)
        for copy in copies:
            copy.wait()
        total = ps[step, 0]
        for v in range(1, nvel):
            total = total + ps[step, v]
        blank = jnp.zeros((113, cells), F32)
        total = jnp.concatenate([total[0:13], kind_row, kn_row, blank], axis=0)
        sums[step] = total.T
        for side, first in ((0, 0), (1, ny - 2)):
            for layer in range(2):
                y_sums[step, side, layer * nx : (layer + 1) * nx, :] = sums[
                    step, pl.ds(first + layer, nx, stride=ny), :
                ]
        for copy in near_copies(step):
            copy.start()
        return total

    def set_coefficients(total, arg_ref, poly_ref, keep_ref):
        arg, poly, keep = coefficients([total[i : i + 1] for i in range(15)])
        arg_ref[...] = pieces(arg)
        poly_ref[...] = pieces(poly)
        keep_ref[...] = jnp.broadcast_to(keep, (LANES, keep.shape[1])).T

    def relax(j):
        wide = phi_ref[j]
        for r in range(0, cells, 128):
            rows = pl.ds(r, 128)
            arg = jnp.dot(arg_c[rows, :], wide, preferred_element_type=F32)
            poly = jnp.dot(poly_c[rows, :], wide, preferred_element_type=F32)
            val = f[j, r // ny : (r + 128) // ny].reshape(128, LANES)
            new = val * keep_c[rows, :] + jnp.exp(arg) * poly
            for i in range(128 // ny):
                g[j, face(r // ny + i + 2), :] = new[i * ny : (i + 1) * ny]

    def relax_halo(step, j):
        wide = phi_ref[j]
        rows = pl.ds(0, halo)
        arg = jnp.dot(arg_h[rows, :], wide, preferred_element_type=F32)
        poly = jnp.dot(poly_h[rows, :], wide, preferred_element_type=F32)
        far_lo = xh[step, j, 0]
        far_hi = far_lo if nsx == 2 else xh[step, j, 3]
        val = jnp.concatenate(
            [far_lo, xh[step, j, 1], xh[step, j, 2], far_hi, yh[step, j, 0], yh[step, j, 1]], axis=0
        )
        new = val * keep_h[rows, :] + jnp.exp(arg) * poly
        for i, slab in enumerate((0, 1, nx + 2, nx + 3)):
            g[j, face(slab), :] = new[i * ny : (i + 1) * ny]
        for i, first in enumerate((-2, -1, ny, ny + 1)):
            at = 4 * ny + i * nx
            g[j, pl.ds(2 * PITCH + TOP + first, nx, stride=PITCH), :] = new[at : at + nx]

    def transport(j):
        half = ny // 2
        lanes = [jnp.broadcast_to(lane_ref[j, i : i + 1, :], (half, LANES)) for i in range(4)]
        pos_x, pos_y = lanes[0] > 0.0, lanes[1] > 0.0
        side_x = jnp.where(pos_x, 0.5, -0.5)
        rate_x, rate_y = lanes[2:]
        for row in (0, half):

            def cells_at(x, d=0):
                return g[j, pl.ds((x + 2) * PITCH + TOP + row + d, half), :]

            low, mid = cells_at(-2), cells_at(-1)
            diff = mid - low
            kept = face_value = flux = None
            for x in range(-1, nx + 1):
                high = cells_at(x + 1)
                ahead = high - mid
                slope = jnp.minimum(
                    jnp.maximum(ahead, jnp.minimum(diff, 0.0)), jnp.maximum(diff, 0.0)
                )
                value = mid + side_x * slope
                if x >= 0:
                    new_flux = jnp.where(pos_x, face_value, value)
                if x >= 1:
                    along = [cells_at(x - 1, d) for d in (-2, -1, 1, 2)]
                    div_y = upwind(pos_y, along[0], along[1], kept, along[2], along[3])
                    f[j, x - 1, row : row + half, :] = kept - (
                        rate_x * (new_flux - flux) + rate_y * div_y
                    )
                if x >= 0:
                    flux = new_flux
                kept, face_value, mid, diff = mid, value, high, ahead

    def send(step, k):
        for copy in halo_copies(step, k):
            copy.start()

    def prepare(k):
        @pl.loop(0, group)
        def _(i):
            j = k * group + i
            build_tables(j)
            in_copy(j).wait()
            pack(j)

    prepare(0)
    pl.semaphore_wait(barrier, len(partners))

    @pl.loop(0, groups)
    def _(k):
        @pl.when(k > 0)
        def _():
            prepare(k)

        @pl.when(k < head)
        def _():
            send(0, k)

        @pl.loop(0, group)
        def _(i):
            add_moments(k * group + i)

    for copy in cell_copies:
        copy.wait()
    kind = kind_ref[...].astype(F32)
    kn = kn_ref[...]
    kind_row = jnp.concatenate([kind[x : x + 1] for x in range(nx)], axis=1)
    kn_row = jnp.concatenate([kn[x : x + 1] for x in range(nx)], axis=1)

    for step in range(STEPS):
        last = step == STEPS - 1
        total = exchange(step)

        @pl.loop(head, groups - 1)
        def _(k):
            send(step, k)

        for i in range(group):
            for copy in halo_copies(step, groups - 1, i):
                copy.start()

        set_coefficients(total, arg_c, poly_c, keep_c)

        @pl.loop(0, ncol)
        def _(j):
            relax(j)

        for copy in near_copies(step):
            copy.wait()
        around = [near[step, 0:halo, :]]
        if halo_pad > halo:
            around.append(sums[step, 0 : halo_pad - halo, :])
        set_coefficients(jnp.concatenate(around, axis=0).T, arg_h, poly_h, keep_h)
        if not last:
            acc[...] = jnp.zeros_like(acc)

        @pl.loop(0, groups - 1)
        def _(k):
            for copy in halo_copies(step, k):
                copy.wait()

            @pl.loop(0, group)
            def _(i):
                j = k * group + i
                relax_halo(step, j)
                transport(j)
                if last:
                    out_copy(j).start()
                else:
                    pack(j)

            if not last:
                @pl.when(k < head)
                def _():
                    send(step + 1, k)

                @pl.loop(0, group)
                def _(i):
                    add_moments(k * group + i)

        @pl.loop(0, group)
        def _(i):
            for copy in halo_copies(step, groups - 1, i):
                copy.wait()
            j = (groups - 1) * group + i
            relax_halo(step, j)
            transport(j)
            if last:
                out_copy(j).start()
            else:
                pack(j)
                add_moments(j)

    @pl.loop(0, ncol)
    def _(j):
        out_copy(j).wait()


def body(sizes, distribution, cell_kind, local_knudsen):
    nx, ny, count = distribution.shape
    ncol = -(-count // LANES)
    width = ncol * LANES
    padded = distribution
    if width != count:
        padded = jnp.pad(distribution, ((0, 0), (0, 0), (0, width - count)))
    group = 3 if ncol % 3 == 0 else 1
    groups, cells = ncol // group, nx * ny
    halo_pad = -(-4 * (nx + ny) // LANES) * LANES
    head = min((4 * groups + 8) // 9, groups - 1)
    nsx, nsy, nvel = sizes
    xcopies = 3 if nsx == 2 else 4
    dma = pltpu.SemaphoreType.DMA
    operands = [
        pltpu.with_memory_space_constraint(a, pltpu.MemorySpace.HBM)
        for a in (padded, cell_kind, local_knudsen)
    ]
    result = pl.pallas_call(
        functools.partial(kernel, sizes, group, head, count),
        out_shape=jax.ShapeDtypeStruct((nx, ny, width), F32),
        in_specs=[pl.BlockSpec(memory_space=pltpu.MemorySpace.HBM)] * 3,
        out_specs=pl.BlockSpec(memory_space=pl.ANY),
        scratch_shapes=[
            pltpu.VMEM((nx, ny), jnp.int32),
            pltpu.VMEM((nx, ny), F32),
            pltpu.VMEM((ncol, nx, ny, LANES), F32),
            pltpu.VMEM((ncol, (nx + 4) * PITCH, LANES), F32),
            pltpu.VMEM((ncol, 3, ny, LANES), F32),
            pltpu.VMEM((ncol, 2, 2 * nx, LANES), F32),
            pltpu.VMEM((STEPS, ncol, xcopies, ny, LANES), F32),
            pltpu.VMEM((STEPS, ncol, 2, 2 * nx, LANES), F32),
            pltpu.VMEM((cells, LANES), F32),
            pltpu.VMEM((ncol, LANES, LANES), BF16),
            pltpu.VMEM((ncol, 8, LANES), F32),
            pltpu.VMEM((cells, LANES), BF16),
            pltpu.VMEM((cells, LANES), BF16),
            pltpu.VMEM((cells, LANES), F32),
            pltpu.VMEM((halo_pad, LANES), BF16),
            pltpu.VMEM((halo_pad, LANES), BF16),
            pltpu.VMEM((halo_pad, LANES), F32),
            pltpu.VMEM((STEPS, nvel, 16, cells), F32),
            pltpu.VMEM((STEPS, cells, LANES), F32),
            pltpu.VMEM((STEPS, 2, 2 * nx, LANES), F32),
            pltpu.VMEM((STEPS, 4 * (nx + ny), LANES), F32),
            dma((2,)),
            dma((ncol,)),
            dma((ncol,)),
            dma((STEPS, groups + group - 1, 3 if nsx == 2 else 6)),
            dma((STEPS, groups + group - 1, 3 if nsx == 2 else 6)),
            dma((STEPS, nvel)),
            dma((STEPS, nvel)),
            dma((STEPS, 4)),
            dma((STEPS, 4)),
        ],
        compiler_params=pltpu.CompilerParams(
            collective_id=0, has_side_effects=True, vmem_limit_bytes=40 * 2**20
        ),
    )(*operands)
    return result[..., :count] if width != count else result


def solution(mesh):
    sizes = (mesh.shape["sx"], mesh.shape["sy"], mesh.shape["vel"])
    return jax.shard_map(
        functools.partial(body, sizes),
        mesh=mesh,
        in_specs=(P("sx", "sy", "vel"), P("sx", "sy"), P("sx", "sy")),
        out_specs=P("sx", "sy", "vel"),
        check_vma=False,
    )
```
